256 devices in a mesh: blk: 64 (over y_hi, x, z), rows: 4 (over y_lo, core).
Axes of the slice: x: 4, y: 4 (y_hi: 2, y_lo: 2; y = y_hi * 2 + y_lo), z: 8, core: 2. Of those that a mesh axis runs over, the one named last changes fastest.
Arguments:
- factor_cols: float32 [16384, 8192], P('rows', 'blk'), may hold values from -1 to 1
- basis_cols: float32 [16384, 8192], P('rows', 'blk'), may hold values from -0.046875 to 0.046875
- samples: float32 [128, 16384], P(None, 'rows'), may hold values from -8 to 8
- pairing: int32 [3, 8, 128], replicated, may hold values from 0 to 127, each once within a row
Outputs:
- eigen_sums: float32 [8192], P('blk')
- corrected: float32 [8192], P('blk')
The draws below stay inside these ranges and needn't reach their ends.
Inputs may be any that keep to these rules, and one draw needn't show every extreme that they name: Each pairing[r, s] lists every number 0 to 127 exactly once.
All inputs are finite; a program needn't handle non-finite values.
Results may differ from the reference program's by a relative error of at most 0.0003.
Values sent between devices are 32-bit elements; how exact they have to be, the bound alone decides.
No kernel may reach another device: no remote copies, remote signals or barrier semaphores. Data moves between devices by JAX's collectives and lax.ppermute only.
A program may use at most 128 MiB of HBM per device.

```python
import math
import jax
import jax.numpy as jnp
from jax import lax

M = 16384
BLOCK = 64
ROUNDS = 3
STEPS = 8
NEX = 128
NCOL = 8192


def draw_factor_cols(key, part):
    key = jax.random.fold_in(key, 17)
    key_noise, key_rows, key_cols = jax.random.split(key, 3)
    rising_rows = jnp.exp(math.log(3.0) * jnp.arange(M, dtype=jnp.float32) / M)
    row_scale = jnp.exp(jax.random.uniform(key_rows, (M,), jnp.float32, 0.0, math.log(10.0))) * rising_rows
    col_scale = jnp.exp(jax.random.uniform(key_cols, (NCOL,), jnp.float32, math.log(0.3), math.log(3.0)))
    noise = jnp.clip(jax.random.normal(key_noise, (M, NCOL), jnp.float32), -6.0, 6.0)
    values = noise * row_scale[:, None] * col_scale[None, :] / math.sqrt(80.0 * M)
    return jnp.clip(values, -1.0, 1.0)


def draw_samples(key, part):
    key = jax.random.fold_in(key, 29)
    key_noise, key_rows, key_feats = jax.random.split(key, 3)
    rising_feats = jnp.exp(math.log(3.0) * jnp.arange(M, dtype=jnp.float32) / M)
    sample_scale = jnp.exp(jax.random.uniform(key_rows, (NEX,), jnp.float32, 0.0, math.log(10.0)))
    feat_scale = jnp.exp(jax.random.uniform(key_feats, (M,), jnp.float32, 0.0, math.log(10.0))) * rising_feats
    noise = jnp.clip(jax.random.normal(key_noise, (NEX, M), jnp.float32), -6.0, 6.0)
    values = noise * sample_scale[:, None] * feat_scale[None, :] / 38.0
    return jnp.clip(values, -8.0, 8.0)


def steps_of(own_key, shape, cuts, low, top_value):
    gain, own = 1.0, jax.random.fold_in(own_key, 6)
    for position, shards_of in cuts:
        steps = jnp.exp(jax.random.uniform(jax.random.fold_in(own, position), (shards_of,), jnp.float32, low / len(cuts), top_value / len(cuts)))
        gain = gain * jnp.repeat(steps, shape[position] // shards_of).reshape([-1 if axis == position else 1 for axis in range(len(shape))])
    return gain


def bell_draw(rng, extent, scale, most, pieces=(), held_as=jnp.bfloat16):
    values = scale * jax.random.normal(rng, extent, jnp.float32)
    if pieces:
        values = values * steps_of(rng, extent, pieces, -0.22, 0.18)
    return jnp.clip(values, -most, most).astype(held_as)


def setup_inputs(seed: int = 0) -> dict:
    key_of = jax.random.split(jax.random.key(seed), 5)
    factor_cols = draw_factor_cols(jax.random.fold_in(key_of[4], 71), 0)
    basis_cols = bell_draw(key_of[1], (M, NCOL), M ** -0.5, 0.046875, ((0, 4), (1, 64)), jnp.float32)
    samples = draw_samples(jax.random.fold_in(key_of[4], 71), 0)
    pairing = jax.vmap(lambda own: jax.random.permutation(own, 2 * BLOCK))(jax.random.split(key_of[3], ROUNDS * STEPS)).reshape((ROUNDS, STEPS, 2 * BLOCK)).astype(jnp.int32)
    return dict(factor_cols=factor_cols, basis_cols=basis_cols, samples=samples, pairing=pairing)


highest = lax.Precision.HIGHEST


def small_solve(gram_pair, order_rows):
    breadth = gram_pair.shape[0]
    half_width = breadth // 2
    settled = gram_pair
    turned = jnp.eye(breadth, dtype=jnp.float32)
    for step_index in range(order_rows.shape[0]):
        order_row = order_rows[step_index]
        chooser = jax.nn.one_hot(order_row, breadth, dtype=jnp.float32)
        permute = jnp.concatenate([chooser[0::2], chooser[1::2]], 0)
        rearranged = jnp.dot(jnp.dot(permute, settled, precision=highest), permute.T, precision=highest)
        diag_first = jnp.diagonal(rearranged[:half_width, :half_width])
        diag_second = jnp.diagonal(rearranged[half_width:, half_width:])
        crossing = jnp.diagonal(rearranged[:half_width, half_width:])
        angles = 0.5 * jnp.arctan2(2.0 * crossing, diag_first - diag_second)
        cosine = jnp.cos(angles)
        sines = jnp.sin(angles)
        core_block = jnp.block([[jnp.diag(cosine), -jnp.diag(sines)], [jnp.diag(sines), jnp.diag(cosine)]])
        rotation = jnp.dot(jnp.dot(permute.T, core_block, precision=highest), permute, precision=highest)
        settled = jnp.dot(jnp.dot(rotation.T, settled, precision=highest), rotation, precision=highest)
        turned = jnp.dot(turned, rotation, precision=highest)
    return turned


def advance(blocks):
    pair_count = blocks.shape[1]
    top_blocks = blocks[:, :, :BLOCK]
    bottom_blocks = blocks[:, :, BLOCK:]
    new_top = jnp.concatenate([top_blocks[:, :1], bottom_blocks[:, :1], top_blocks[:, 1:pair_count - 1]], axis=1)
    new_bottom = jnp.concatenate([bottom_blocks[:, 1:], top_blocks[:, pair_count - 1:]], axis=1)
    return jnp.concatenate([new_top, new_bottom], axis=2)


def reference(factor_cols, basis_cols, samples, pairing):
    pair_count = NCOL // (2 * BLOCK)
    factor_now = factor_cols.reshape(M, pair_count, 2 * BLOCK)
    basis_now = basis_cols.reshape(M, pair_count, 2 * BLOCK)
    for round_index in range(ROUNDS):
        grams = jnp.einsum("mpi,mpj->pij", factor_now, factor_now, precision=highest)
        turns = jax.vmap(small_solve, in_axes=(0, None))(grams, pairing[round_index])
        factor_now = jnp.einsum("mpi,pij->mpj", factor_now, turns, precision=highest)
        basis_now = jnp.einsum("mpi,pij->mpj", basis_now, turns, precision=highest)
        factor_now = advance(factor_now)
        basis_now = advance(basis_now)
    factor_final = factor_now.reshape(M, NCOL)
    basis_final = basis_now.reshape(M, NCOL)
    eigen_sums = jnp.sum(factor_final * factor_final, axis=0)
    projected = jnp.dot(samples, basis_final, precision=highest, preferred_element_type=jnp.float32)
    corrected = jnp.mean(projected * projected, axis=0)
    return (eigen_sums, corrected)
```

```python
import jax
import jax.numpy as jnp
from jax import lax
from jax.experimental import pallas as pl
from jax.experimental.pallas import tpu as pltpu
from jax.sharding import PartitionSpec as P

f32 = jnp.float32
bf16 = jnp.bfloat16
VMEM = pl.BlockSpec(memory_space=pltpu.VMEM)
SMEM = pl.BlockSpec(memory_space=pltpu.SMEM)
params = pltpu.CompilerParams(vmem_limit_bytes=40 * 1024 * 1024)


def split(value):
    high = value.astype(bf16)
    low = (value - high.astype(f32)).astype(bf16)
    return high, low


def dot(left, right):
    return jnp.dot(left, right, preferred_element_type=f32)


def dot_rows(left, right):
    return lax.dot_general(left, right, (((0,), (0,)), ((), ())), preferred_element_type=f32)


def dot_fine(left, right):
    return jnp.dot(left, right, precision=lax.Precision.HIGHEST, preferred_element_type=f32)


def rotated(left, right_high, right_low):
    high, low = split(left)
    return dot(high, right_high) + dot(low, right_high) + dot(high, right_low)


def chunks_of(rows, most):
    size = min(rows, most)
    return rows // size, size


def call(body, out_shape, in_specs, scratch=(), cost=None):
    outs = jax.tree.map(lambda _: VMEM, out_shape)
    return pl.pallas_call(
        body,
        out_shape=out_shape,
        in_specs=in_specs,
        out_specs=outs,
        scratch_shapes=list(scratch),
        compiler_params=params,
        cost_estimate=cost,
    )


def shape(*dims):
    return jax.ShapeDtypeStruct(dims, f32)


def first_gram_body(factor_ref, out_ref):
    count, size = chunks_of(factor_ref.shape[0], 1024)
    width = factor_ref.shape[1]

    def step(i, total):
        high, low = split(factor_ref[pl.ds(pl.multiple_of(i * size, size), size), :])
        return total + dot_rows(high, jnp.concatenate([high, low], 1))

    total = lax.fori_loop(0, count, step, jnp.zeros((width, 2 * width), f32))
    cross = total[:, width:]
    out_ref[...] = total[:, :width] + (cross + cross.T)


def project_body(samples_ref, basis_ref, out_ref):
    count, size = chunks_of(basis_ref.shape[0], 1024)

    def step(i, total):
        rows = pl.ds(pl.multiple_of(i * size, size), size)
        left_high, left_low = split(samples_ref[:, rows])
        right_high, right_low = split(basis_ref[rows, :])
        both = dot(left_high, jnp.concatenate([right_high, right_low], 1))
        width = right_high.shape[1]
        return total + both[:, :width] + both[:, width:] + dot(left_low, right_high)

    out_ref[...] = lax.fori_loop(0, count, step, jnp.zeros(out_ref.shape, f32))


def diagonal_of(value, eye):
    return jnp.sum(jnp.where(eye, value, 0.0), axis=0, keepdims=True)


def lanes(value, index):
    return jnp.take_along_axis(value, index, axis=1, mode="promise_in_bounds")


def solve(settled, carried, partner_ref, sign_ref):
    width = settled.shape[0]
    row_id = lax.broadcasted_iota(jnp.int32, (width, width), 0)
    col_id = lax.broadcasted_iota(jnp.int32, (width, width), 1)
    eye = row_id == col_id
    for step in range(partner_ref.shape[0]):
        sign = sign_ref[step : step + 1, :]
        index = jnp.broadcast_to(partner_ref[step : step + 1, :], (width, width))
        swapped = lanes(settled, index)
        own = diagonal_of(settled, eye)
        crossing = diagonal_of(swapped, eye)
        both = lanes(
            jnp.concatenate([jnp.broadcast_to(own, (8, width)), jnp.broadcast_to(crossing, (8, width))], 0),
            index[:16],
        )
        across = sign * (own - both[0:1])
        up = crossing + both[8:9]
        scale = jnp.maximum(jnp.abs(across), jnp.abs(up))
        safe = jnp.where(scale > 0.0, scale, 1.0)
        across = jnp.where(scale > 0.0, across / safe, 1.0)
        up = up / safe
        hypot = jnp.sqrt(across * across + up * up)
        major = jnp.sqrt(0.5 + 0.5 * jnp.abs(across) / hypot)
        minor = 0.5 * jnp.abs(up) / (hypot * major)
        ahead = across >= 0.0
        cosine = jnp.where(ahead, major, minor)
        sine = jnp.where(ahead, minor, major)
        sine = jnp.where(up < 0.0, -sine, sine) * sign
        turned = settled * cosine + swapped * sine
        turned = turned.T
        settled = turned * cosine + lanes(turned, index) * sine
        carried = carried * cosine + lanes(carried, index) * sine
    return settled, carried, eye


def first_solve_body(own_ref, other_ref, partner_ref, sign_ref, turn_ref):
    gram = own_ref[...] + other_ref[...]
    width = gram.shape[0]
    row_id = lax.broadcasted_iota(jnp.int32, (width, width), 0)
    col_id = lax.broadcasted_iota(jnp.int32, (width, width), 1)
    identity = jnp.where(row_id == col_id, 1.0, 0.0).astype(f32)
    settled, turn, _ = solve(gram, identity, partner_ref, sign_ref)
    turn_ref[...] = turn


def rotate_body(place_ref, factor_ref, projected_ref, turn_ref, rise_ref, fall_ref):
    width = factor_ref.shape[1]
    half = width // 2
    packed = factor_ref.shape[0] // 2
    count, size = chunks_of(packed, 512)
    turn = turn_ref[...]
    swapped = jnp.concatenate([turn[:, half:], turn[:, :half]], 1)
    turn = jnp.where(place_ref[0] == 0, swapped, turn)
    rising, falling = turn[:, :half], turn[:, half:]
    empty = jnp.zeros_like(rising)
    weights = jnp.concatenate(
        [
            jnp.concatenate([rising, empty, falling, empty], 1),
            jnp.concatenate([empty, rising, empty, falling], 1),
        ],
        0,
    )
    weights_high, weights_low = split(weights)

    def step(i, _):
        start = pl.multiple_of(i * size, size)
        rows = pl.ds(start, size)
        left = jnp.concatenate(
            [factor_ref[rows, :], factor_ref[pl.ds(pl.multiple_of(packed + start, size), size), :]], 1
        )
        result = rotated(left, weights_high, weights_low)
        rise_ref[rows, :] = result[:, :width]
        fall_ref[rows, :] = result[:, width:]
        return 0

    lax.fori_loop(0, count, step, 0)
    extra = projected_ref.shape[0] // 2
    left = jnp.concatenate([projected_ref[:extra, :], projected_ref[extra:, :]], 1)
    result = rotated(left, weights_high, weights_low)
    rise_ref[packed : packed + extra, :] = result[:, :width]
    fall_ref[packed : packed + extra, :] = result[:, width:]


def folded(whole):
    half = whole.shape[0] // 4

    def block(i, j):
        return whole[i * half : (i + 1) * half, j * half : (j + 1) * half]

    return jnp.concatenate(
        [
            jnp.concatenate([block(0, 0) + block(1, 1), block(0, 2) + block(1, 3)], 1),
            jnp.concatenate([block(2, 0) + block(3, 1), block(2, 2) + block(3, 3)], 1),
        ],
        0,
    )


def second_gram_body(rows, top_ref, bottom_ref, out_ref):
    count, size = chunks_of(rows, 512)
    width = 2 * top_ref.shape[1]

    def step(i, total):
        part = pl.ds(pl.multiple_of(i * size, size), size)
        high, low = split(jnp.concatenate([top_ref[part, :], bottom_ref[part, :]], 1))
        return total + dot_rows(high, jnp.concatenate([high, low], 1))

    total = lax.fori_loop(0, count, step, jnp.zeros((width, 2 * width), f32))
    cross = folded(total[:, width:])
    out_ref[...] = folded(total[:, :width]) + (cross + cross.T)


def second_solve_body(place_ref, own_ref, other_ref, partner_ref, sign_ref, up_ref, down_ref):
    gram = own_ref[...] + other_ref[...]
    width = gram.shape[0]
    half = width // 2
    row_id = lax.broadcasted_iota(jnp.int32, (width, width), 0)
    col_id = lax.broadcasted_iota(jnp.int32, (width, width), 1)
    identity = jnp.where(row_id == col_id, 1.0, 0.0).astype(f32)
    settled, turn, _ = solve(gram, identity, partner_ref, sign_ref)
    empty = jnp.zeros((half, half), f32)
    top = jnp.concatenate(
        [turn[:, :half], jnp.concatenate([settled[:half, :half], empty], 0)], 1
    )
    bottom = jnp.concatenate(
        [turn[:, half:], jnp.concatenate([settled[half:, half:], empty], 0)], 1
    )
    at_first = place_ref[0] == 0
    up_ref[...] = jnp.where(at_first, bottom, top)
    down_ref[...] = jnp.where(at_first, top, bottom)


def cross_body(
    rows, final, place_ref, rise_ref, fall_ref, low1_ref, high1_ref, low2_ref, high2_ref,
    left_ref, right_ref, out_ref,
):
    width = rise_ref.shape[1]
    half = width // 2
    count, size = chunks_of(rows, 512)
    at_first = place_ref[0] == 0
    at_last = place_ref[0] == final

    def sides(part):
        rise = rise_ref[part, :]
        fall = fall_ref[part, :]
        left = jnp.concatenate(
            [
                jnp.where(at_first, fall, low2_ref[part, :]),
                jnp.where(at_first, high1_ref[part, :], fall),
            ],
            1,
        )
        right = jnp.concatenate(
            [
                jnp.where(at_last, low1_ref[part, :], rise),
                jnp.where(at_last, rise, high2_ref[part, :]),
            ],
            1,
        )
        return left, right

    def step(i, total):
        left, right = sides(pl.ds(pl.multiple_of(i * size, size), size))
        left_high, left_low = split(left)
        right_high, right_low = split(right)
        return total + (
            dot_rows(left_high, right_high)
            + dot_rows(left_high, right_low)
            + dot_rows(left_low, right_high)
        )

    total = lax.fori_loop(0, count, step, jnp.zeros((2 * width, 2 * width), f32))
    cross = folded(total)
    left_turn = left_ref[:, :half]
    right_turn = right_ref[:, :half]
    cross = dot_fine(dot_fine(left_turn.T, cross), right_turn)
    extra = rise_ref.shape[0] - rows
    left, right = sides(slice(rows, rows + extra))

    def unpacked(value):
        return jnp.concatenate(
            [
                jnp.concatenate([value[:, :half], value[:, width : width + half]], 1),
                jnp.concatenate([value[:, half:width], value[:, width + half :]], 1),
            ],
            0,
        )

    out_ref[: 2 * extra, :half] = dot_fine(unpacked(left), left_turn)
    out_ref[: 2 * extra, half:] = dot_fine(unpacked(right), right_turn)
    out_ref[2 * extra :, :half] = cross
    out_ref[2 * extra :, half:] = jnp.zeros_like(cross)


def last_solve_body(own_ref, other_ref, left_ref, right_ref, partner_ref, sign_ref, out_ref):
    whole = own_ref[...] + other_ref[...]
    width = whole.shape[1]
    half = width // 2
    rows = whole.shape[0] - half
    cross = whole[rows:, :half]
    gram = jnp.concatenate(
        [
            jnp.concatenate([left_ref[:half, half:], cross], 1),
            jnp.concatenate([cross.T, right_ref[:half, half:]], 1),
        ],
        0,
    )
    settled, projected, eye = solve(gram, whole[:rows], partner_ref, sign_ref)
    squares = jnp.sum(projected * projected, axis=0, keepdims=True) * (1.0 / rows)
    sums = diagonal_of(settled, eye)
    out_ref[...] = jnp.concatenate([sums, squares, jnp.zeros((6, width), f32)], 0)


def shifted(value, steps):
    count = lax.axis_size("blk")
    leading, last = (max(0, -steps), min(count, count - steps))
    return lax.ppermute(value, "blk", [(i, i + steps) for i in range(leading, last)])


def flipped(value, bit):
    return lax.ppermute(value, "rows", [(i, i ^ bit) for i in range(lax.axis_size("rows"))])


def partial_sums(value):
    paired = value + flipped(value, 1)
    return paired, flipped(paired, 2)


def partners_of(pairing):
    width = pairing.shape[-1]
    hits = pairing[..., :, None] == jnp.arange(width, dtype=jnp.int32)
    swapped = pairing.reshape(*pairing.shape[:-1], width // 2, 2)[..., ::-1].reshape(pairing.shape)
    partner = jnp.sum(jnp.where(hits, swapped[..., :, None], 0), axis=-2)
    signs = jnp.where(jnp.arange(width) % 2 == 0, 1.0, -1.0).astype(f32)
    sign = jnp.sum(jnp.where(hits, signs[:, None], 0.0), axis=-2)
    return partner, sign


def on_device(factor_cols, basis_cols, samples, pairing):
    width = factor_cols.shape[1]
    half = width // 2
    packed = factor_cols.shape[0] // 2
    sample_count = samples.shape[0]
    long = packed + sample_count // 2
    position = lax.axis_index("blk")
    final = lax.axis_size("blk") - 1
    at_first = position == 0
    at_last = position == final
    place = position.astype(jnp.int32).reshape(1)
    partner, sign = partners_of(pairing)

    gram = call(first_gram_body, shape(width, width), [VMEM])(factor_cols)
    own, other = partial_sums(gram)
    projected = call(project_body, shape(sample_count, width), [VMEM, VMEM])(samples, basis_cols)
    turn = call(first_solve_body, shape(width, width), [VMEM] * 4)(own, other, partner[0], sign[0])
    rise, fall = call(rotate_body, (shape(long, width), shape(long, width)), [SMEM] + [VMEM] * 3)(
        place, factor_cols, projected, turn
    )
    low1 = shifted(rise, 1)
    high1 = shifted(fall, -1)
    top = jnp.where(at_first, fall, low1)
    bottom = jnp.where(at_last, rise, high1)
    low2 = shifted(top, 1)
    high2 = shifted(bottom, -1)
    gram = call(lambda *refs: second_gram_body(packed, *refs), shape(width, width), [VMEM] * 2)(top, bottom)
    own, other = partial_sums(gram)
    up, down = call(second_solve_body, (shape(width, width), shape(width, width)), [SMEM] + [VMEM] * 4)(
        place, own, other, partner[1], sign[1]
    )
    from_low = shifted(up, 1)
    from_high = shifted(down, -1)
    left = jnp.where(at_first, down, from_low)
    right = jnp.where(at_last, up, from_high)
    whole = call(
        lambda *refs: cross_body(packed, final, *refs),
        shape(sample_count + half, width),
        [SMEM] + [VMEM] * 8,
    )(place, rise, fall, low1, high1, low2, high2, left, right)
    own, other = partial_sums(whole)
    result = call(last_solve_body, shape(8, width), [VMEM] * 6)(
        own, other, left, right, partner[2], sign[2]
    )
    from_low = shifted(result, 1)
    from_high = shifted(result, -1)
    lower = jnp.where(
        at_first, result[:2, :half], jnp.where(position == 1, from_low[:2, half:], from_low[:2, :half])
    )
    upper = jnp.where(at_last, result[:2, :half], from_high[:2, half:])
    both = jnp.concatenate([lower, upper], 1)
    return (both[0], both[1])


def solution(mesh):
    in_specs = (P("rows", "blk"), P("rows", "blk"), P(None, "rows"), P())
    out_specs = (P("blk"), P("blk"))
    return jax.shard_map(
        on_device, mesh=mesh, in_specs=in_specs, out_specs=out_specs, check_vma=False
    )
```

```python
import jax
import jax.numpy as jnp
from jax import lax
from jax.experimental import pallas as pl
from jax.experimental.pallas import tpu as pltpu
from jax.sharding import PartitionSpec as P

f32 = jnp.float32
bf16 = jnp.bfloat16
i32 = jnp.int32
VMEM = pl.BlockSpec(memory_space=pltpu.VMEM)
params = pltpu.CompilerParams(vmem_limit_bytes=24 * 1024 * 1024)
PIECES = 1


def split(value):
    high = value.astype(bf16)
    low = (value - high.astype(f32)).astype(bf16)
    return high, low


def dot(left, right):
    return jnp.dot(left, right, preferred_element_type=f32)


def dot_rows(left, right):
    return lax.dot_general(left, right, (((0,), (0,)), ((), ())), preferred_element_type=f32)


def dot_fine(left, right):
    return jnp.dot(left, right, precision=lax.Precision.HIGHEST, preferred_element_type=f32)


def rotated(left, right):
    high, low = split(left)
    return dot(jnp.concatenate([high, low, high], 1), right)


def stacked(right):
    high, low = split(right)
    return jnp.concatenate([high, high, low], 0)


def chunks_of(rows, most):
    size = min(rows, most)
    return rows // size, size


def rows_at(index, size):
    return pl.ds(pl.multiple_of(index * size, size), size)


def call(body, out_shape, in_specs):
    return pl.pallas_call(
        body,
        out_shape=out_shape,
        in_specs=in_specs,
        out_specs=jax.tree.map(lambda _: VMEM, out_shape),
        compiler_params=params,
    )


def shape(*dims, dtype=f32):
    return jax.ShapeDtypeStruct(dims, dtype)


def swapped_rows(value):
    half = value.shape[0] // 2
    return jnp.concatenate([value[half:], value[:half]], 0)


def swapped_cols(value):
    half = value.shape[1] // 2
    return jnp.concatenate([value[:, half:], value[:, :half]], 1)


def first_gram_body(factor_ref, out_ref, total_ref):
    width = factor_ref.shape[1]
    step = pl.program_id(0)
    high, low = split(factor_ref[...])
    part = dot_rows(high, jnp.concatenate([high, low], 1))

    @pl.when(step == 0)
    def _():
        total_ref[...] = part

    @pl.when(step > 0)
    def _():
        total_ref[...] += part

    @pl.when(step == pl.num_programs(0) - 1)
    def _():
        total = total_ref[...]
        cross = total[:, width:]
        out_ref[...] = total[:, :width] + (cross + cross.T)


def first_gram(factor_cols):
    rows, width = factor_cols.shape
    count, size = chunks_of(rows, 1024)
    return pl.pallas_call(
        first_gram_body,
        out_shape=shape(width, width),
        grid=(count,),
        in_specs=[pl.BlockSpec((size, width), lambda i: (i, 0))],
        out_specs=pl.BlockSpec((width, width), lambda i: (0, 0)),
        scratch_shapes=[pltpu.VMEM((width, 2 * width), f32)],
        compiler_params=params,
    )(factor_cols)


def project_body(samples_ref, basis_ref, order_ref, out_ref, partner_ref, sign_ref):
    width = basis_ref.shape[1]
    count, size = chunks_of(basis_ref.shape[0], 1024)

    def step(i, total):
        rows = rows_at(i, size)
        left_high, left_low = split(samples_ref[:, rows])
        right_high, right_low = split(basis_ref[rows, :])
        both = dot(left_high, jnp.concatenate([right_high, right_low], 1))
        return total + both[:, :width] + both[:, width:] + dot(left_low, right_high)

    out_ref[...] = lax.fori_loop(0, count, step, jnp.zeros(out_ref.shape, f32))

    lines = order_ref.shape[0]
    order = order_ref[...]
    lane = lax.broadcasted_iota(i32, (lines, width), 1)
    ahead = jnp.concatenate([order[:, 1:], order[:, :1]], 1)
    behind = jnp.concatenate([order[:, -1:], order[:, :-1]], 1)
    even = lane % 2 == 0
    other = jnp.where(even, ahead, behind + width)
    filler = jnp.zeros((width - lines, width), i32)
    order = jnp.concatenate([order, filler], 0).T
    other = jnp.concatenate([other, filler], 0).T
    column = lax.broadcasted_iota(i32, (width, width), 1)
    found = []
    for line in range(lines):
        hits = jnp.where(order[:, line : line + 1] == column, other[:, line : line + 1], 0)
        found.append(jnp.sum(hits, axis=0, keepdims=True))
    found = jnp.concatenate(found, 0)
    first = found < width
    partner_ref[...] = jnp.where(first, found, found - width)
    sign_ref[...] = jnp.where(first, 1.0, -1.0).astype(f32)


def diagonal_of(value, eye):
    return jnp.sum(jnp.where(eye, value, 0.0), axis=0, keepdims=True)


def lanes(value, index):
    return jnp.take_along_axis(value, index, axis=1, mode="promise_in_bounds")


def eye_of(width):
    row_id = lax.broadcasted_iota(i32, (width, width), 0)
    col_id = lax.broadcasted_iota(i32, (width, width), 1)
    return row_id == col_id


def turn_step(settled, carried, eye, index, sign):
    width = settled.shape[0]
    swapped = lanes(settled, index)
    own = diagonal_of(settled, eye)
    crossing = diagonal_of(swapped, eye)
    both = lanes(
        jnp.concatenate([jnp.broadcast_to(own, (8, width)), jnp.broadcast_to(crossing, (8, width))], 0),
        index[:16],
    )
    across = sign * (own - both[0:1])
    up = crossing + both[8:9]
    scale = jnp.maximum(jnp.abs(across), jnp.abs(up))
    safe = jnp.where(scale > 0.0, scale, 1.0)
    across = jnp.where(scale > 0.0, across / safe, 1.0)
    up = up / safe
    hypot = jnp.sqrt(across * across + up * up)
    major = jnp.sqrt(0.5 + 0.5 * jnp.abs(across) / hypot)
    minor = 0.5 * jnp.abs(up) / (hypot * major)
    ahead = across >= 0.0
    cosine = jnp.where(ahead, major, minor)
    sine = jnp.where(ahead, minor, major)
    sine = jnp.where(up < 0.0, -sine, sine) * sign
    turned = (settled * cosine + swapped * sine).T
    settled = turned * cosine + lanes(turned, index) * sine
    carried = carried * cosine + lanes(carried, index) * sine
    return settled, carried


def solve(problems, partners, signs):
    width = problems[0][0].shape[0]
    eye = eye_of(width)
    for step in range(partners.shape[0]):
        sign = signs[step : step + 1, :]
        index = jnp.broadcast_to(partners[step : step + 1, :], (width, width))
        problems = [turn_step(*problem, eye, index, sign) for problem in problems]
    return problems


def round_of(ref, index, rounds):
    steps = ref.shape[0] // rounds
    return ref[index * steps : (index + 1) * steps, :]


def blk_index():
    return lax.axis_index("blk").astype(i32)


def top_goes_odd():
    position = blk_index()
    return jnp.logical_or(position % 2 == 1, position == 0)


def odd_takes_top(final):
    position = blk_index()
    return jnp.logical_or(position % 2 == 0, position == final)


def even_takes_top():
    position = blk_index()
    return jnp.logical_and(position % 2 == 1, position != 1)


def identity_of(width):
    return jnp.where(eye_of(width), 1.0, 0.0).astype(f32)


def first_solve_body(rounds, own_ref, other_ref, partner_ref, sign_ref, turn_ref):
    gram = own_ref[...] + other_ref[...]
    ((_, turn_ref[...]),) = solve(
        [(gram, identity_of(gram.shape[0]))],
        round_of(partner_ref, 0, rounds),
        round_of(sign_ref, 0, rounds),
    )


def rotate_body(factor_ref, projected_ref, turn_ref, *out_refs):
    odd_refs, even_refs = out_refs[: len(out_refs) // 2], out_refs[len(out_refs) // 2 :]
    width = factor_ref.shape[1]
    half = width // 2
    packed = factor_ref.shape[0] // 2
    turn = turn_ref[...]
    turn = jnp.where(top_goes_odd(), turn, swapped_cols(turn))
    for_odd, for_even = turn[:, :half], turn[:, half:]
    empty = jnp.zeros_like(for_odd)
    weights = jnp.concatenate(
        [
            jnp.concatenate([for_odd, empty, for_even, empty], 1),
            jnp.concatenate([empty, for_odd, empty, for_even], 1),
        ],
        0,
    )
    weights = stacked(weights)
    piece = packed // len(odd_refs)
    count, size = chunks_of(piece, 512)
    for number, (odd_ref, even_ref) in enumerate(zip(odd_refs, even_refs)):

        def step(i, _):
            start = pl.multiple_of(i * size, size)
            lower = pl.ds(pl.multiple_of(number * piece + start, size), size)
            upper = pl.ds(pl.multiple_of(packed + number * piece + start, size), size)
            left = jnp.concatenate([factor_ref[lower, :], factor_ref[upper, :]], 1)
            result = rotated(left, weights)
            odd_ref[pl.ds(start, size), :] = result[:, :width]
            even_ref[pl.ds(start, size), :] = result[:, width:]
            return 0

        lax.fori_loop(0, count, step, 0)
    extra = projected_ref.shape[0] // 2
    left = jnp.concatenate([projected_ref[:extra, :], projected_ref[extra:, :]], 1)
    result = rotated(left, weights)
    odd_refs[-1][piece : piece + extra, :] = result[:, :width]
    even_refs[-1][piece : piece + extra, :] = result[:, width:]


def folded(whole):
    half = whole.shape[0] // 4

    def block(i, j):
        return whole[i * half : (i + 1) * half, j * half : (j + 1) * half]

    return jnp.concatenate(
        [
            jnp.concatenate([block(0, 0) + block(1, 1), block(0, 2) + block(1, 3)], 1),
            jnp.concatenate([block(2, 0) + block(3, 1), block(2, 2) + block(3, 3)], 1),
        ],
        0,
    )


def second_gram_body(piece, *refs):
    refs, out_ref = refs[:-1], refs[-1]
    odd_refs, even_refs = refs[: len(refs) // 2], refs[len(refs) // 2 :]
    count, size = chunks_of(piece, 512)
    width = 2 * odd_refs[0].shape[1]
    total = jnp.zeros((width, 2 * width), f32)
    for odd_ref, even_ref in zip(odd_refs, even_refs):

        def step(i, total):
            part = rows_at(i, size)
            high, low = split(jnp.concatenate([odd_ref[part, :], even_ref[part, :]], 1))
            return total + dot_rows(high, jnp.concatenate([high, low], 1))

        total = lax.fori_loop(0, count, step, total)
    cross = folded(total[:, width:])
    gram = folded(total[:, :width]) + (cross + cross.T)
    out_ref[...] = jnp.where(blk_index() % 2 == 1, swapped_rows(swapped_cols(gram)), gram)


def second_solve_body(rounds, own_ref, other_ref, partner_ref, sign_ref, out_ref):
    gram = own_ref[...] + other_ref[...]
    width = gram.shape[0]
    half = width // 2
    ((settled, turn),) = solve(
        [(gram, identity_of(width))], round_of(partner_ref, 1, rounds), round_of(sign_ref, 1, rounds)
    )
    take_top = jnp.logical_xor(top_goes_odd(), lax.axis_index("rows") % 2 == 1)
    out_ref[:, :half] = jnp.where(take_top, turn[:, :half], turn[:, half:])
    out_ref[:half, half:] = jnp.where(take_top, settled[:half, :half], settled[half:, half:])
    out_ref[half:, half:] = jnp.zeros((half, half), f32)


def cross_body(piece, final, *refs):
    refs, out_ref = refs[:-1], refs[-1]
    number = len(refs) // 5
    odd_far, odd_own, even_own, even_far, even_once = (
        refs[i * number : (i + 1) * number] for i in range(5)
    )
    position = blk_index()
    at_edge = jnp.logical_or(position == 0, position == final)
    width = odd_own[0].shape[1]
    half = width // 2
    count, size = chunks_of(piece, 512)

    def sides(index, part):
        return (
            jnp.concatenate(
                [
                    jnp.where(at_edge, even_once[index][part, :], odd_far[index][part, :]),
                    odd_own[index][part, :],
                ],
                1,
            ),
            jnp.concatenate([even_own[index][part, :], even_far[index][part, :]], 1),
        )

    total = jnp.zeros((2 * width, 2 * width), f32)
    for index in range(number):

        def step(i, total):
            left, right = sides(index, rows_at(i, size))
            left_high, left_low = split(left)
            right_high, right_low = split(right)
            return total + dot_rows(
                jnp.concatenate([left_high, left_high, left_low], 0),
                jnp.concatenate([right_high, right_low, right_high], 0),
            )

        total = lax.fori_loop(0, count, step, total)
    out_ref[:width, :] = folded(total)
    extra = odd_own[-1].shape[0] - piece
    for side, value in enumerate(sides(-1, slice(piece, piece + extra))):
        start = width + side * 2 * extra
        out_ref[start : start + extra, :half] = value[:, :half]
        out_ref[start : start + extra, half:] = value[:, width : width + half]
        out_ref[start + extra : start + 2 * extra, :half] = value[:, half:width]
        out_ref[start + extra : start + 2 * extra, half:] = value[:, width + half :]


def combine_body(final, cross_ref, own_ref, other_ref, out_ref):
    width = cross_ref.shape[1]
    half = width // 2
    count = (cross_ref.shape[0] - width) // 2
    position = blk_index()
    odd = position % 2 == 1
    at_edge = jnp.logical_or(position == 0, position == final)
    first_core = lax.axis_index("rows") % 2 == 0
    from_odd = jnp.where(first_core, own_ref[...], other_ref[...])
    from_even = jnp.where(first_core, other_ref[...], own_ref[...])
    odd_turn, even_turn = from_odd[:, :half], from_even[:, :half]
    odd_turn = jnp.where(jnp.logical_xor(odd, at_edge), swapped_rows(odd_turn), odd_turn)
    even_turn = jnp.where(odd, swapped_rows(even_turn), even_turn)
    cross = dot_fine(dot_fine(odd_turn.T, cross_ref[:width, :]), even_turn)
    cross_turned = cross.T
    share = 0.25
    odd_gram = from_odd[:half, half:] * share
    even_gram = from_even[:half, half:] * share
    odd_samples = dot_fine(cross_ref[width : width + count, :], odd_turn)
    even_samples = dot_fine(cross_ref[width + count :, :], even_turn)
    straight = jnp.concatenate(
        [
            jnp.concatenate([odd_gram, cross], 1),
            jnp.concatenate([cross_turned, even_gram], 1),
            jnp.concatenate([odd_samples, even_samples], 1),
        ],
        0,
    )
    turned = jnp.concatenate(
        [
            jnp.concatenate([even_gram, cross_turned], 1),
            jnp.concatenate([cross, odd_gram], 1),
            jnp.concatenate([even_samples, odd_samples], 1),
        ],
        0,
    )
    out_ref[...] = jnp.where(odd, turned, straight)


def last_solve_body(
    rounds, final, odd_ref, odd_other_ref, even_ref, even_other_ref, partner_ref, sign_ref, sums_ref, squares_ref
):
    wholes = [odd_ref[...] + odd_other_ref[...], even_ref[...] + even_other_ref[...]]
    width = wholes[0].shape[1]
    half = width // 2
    samples = wholes[0].shape[0] - width
    solved = solve(
        [(whole[:width], whole[width:]) for whole in wholes],
        round_of(partner_ref, 2, rounds),
        round_of(sign_ref, 2, rounds),
    )
    takes = [odd_takes_top(final), even_takes_top()]
    halves = []
    for (settled, projected), take_top in zip(solved, takes):
        sums = diagonal_of(settled, eye_of(width))
        squares = jnp.sum(projected * projected, axis=0, keepdims=True) * (1.0 / samples)
        both = jnp.concatenate([sums, squares], 0)
        halves.append(jnp.where(take_top, both[:, :half], both[:, half:]))
    odd = blk_index() % 2 == 1
    first = jnp.where(odd, halves[1], halves[0])
    second = jnp.where(odd, halves[0], halves[1])
    result = jnp.concatenate([first, second], 1)
    sums_ref[...] = result[0:1]
    squares_ref[...] = result[1:2]


def odd_partner(position, count):
    partner = position - 1 if position % 2 == 0 else position + 1
    return partner if 0 <= partner < count else position


def even_partner(position):
    return position + 1 if position % 2 == 0 else position - 1


def via_odd(value, closed):
    count = lax.axis_size("blk")
    pairs = [(i, odd_partner(i, count)) for i in range(count)]
    return lax.ppermute(value, "blk", [pair for pair in pairs if closed or pair[0] != pair[1]])


def via_even(value):
    count = lax.axis_size("blk")
    return lax.ppermute(value, "blk", [(i, even_partner(i)) for i in range(count)])


def both_chips(value, partner_of):
    count, rows = lax.axis_size("blk"), lax.axis_size("rows")
    pairs = []
    for i in range(count):
        for row in range(rows):
            chip, core = row // 2, row % 2
            pairs.append((i * rows + row, partner_of(i) * rows + core * 2 + chip))
    mine = lax.ppermute(value, ("blk", "rows"), pairs)
    return mine, flipped(mine, 1)


def both_partners(value):
    count = lax.axis_size("blk")
    even = both_chips(value, even_partner)
    odd = both_chips(value, lambda i: odd_partner(i, count))
    return odd + even


def by_core(value):
    count, rows = lax.axis_size("blk"), lax.axis_size("rows")
    pairs = []
    for i in range(count):
        for row in range(rows):
            target = even_partner(i) if row % 2 else odd_partner(i, count)
            pairs.append((i * rows + row, target * rows + row))
    return lax.ppermute(value, ("blk", "rows"), pairs)


def flipped(value, bit):
    return lax.ppermute(value, "rows", [(i, i ^ bit) for i in range(lax.axis_size("rows"))])


def on_device(factor_cols, basis_cols, samples, pairing):
    width = factor_cols.shape[1]
    packed = factor_cols.shape[0] // 2
    sample_count = samples.shape[0]
    extra = sample_count // 2
    rounds, steps = pairing.shape[0], pairing.shape[1]
    piece = packed // PIECES
    final = lax.axis_size("blk") - 1

    gram = first_gram(factor_cols)
    paired = gram + flipped(gram, 1)
    pairing, paired = lax.optimization_barrier((pairing, paired))
    projected, partner, sign = call(
        project_body,
        (
            shape(sample_count, width),
            shape(rounds * steps, width, dtype=i32),
            shape(rounds * steps, width),
        ),
        [VMEM] * 3,
    )(samples, basis_cols, pairing.reshape(rounds * steps, width))
    turn = call(lambda *refs: first_solve_body(rounds, *refs), shape(width, width), [VMEM] * 4)(
        paired, flipped(paired, 2), partner, sign
    )
    pieces = [shape(piece + (extra if i == PIECES - 1 else 0), width) for i in range(PIECES)]
    sent = call(rotate_body, tuple(pieces + pieces), [VMEM] * 3)(factor_cols, projected, turn)
    to_odd, to_even = sent[:PIECES], sent[PIECES:]
    odd_once, even_once, odd_twice, even_twice = [], [], [], []
    for i in range(PIECES):
        even_once.append(via_even(to_even[i]))
        odd_once.append(via_odd(to_odd[i], True))
    for i in range(PIECES):
        odd_twice.append(via_odd(even_once[i], False))
        even_twice.append(via_even(odd_once[i]))
    gram = call(lambda *refs: second_gram_body(piece, *refs), shape(width, width), [VMEM] * (2 * PIECES))(
        *odd_once, *even_once
    )
    paired = gram + flipped(gram, 1)
    message = call(lambda *refs: second_solve_body(rounds, *refs), shape(width, width), [VMEM] * 4)(
        paired, flipped(paired, 2), partner, sign
    )
    message = by_core(message)
    message_other = flipped(message, 1)
    cross = call(
        lambda *refs: cross_body(piece, final, *refs),
        shape(width + 2 * sample_count, width),
        [VMEM] * (5 * PIECES),
    )(*odd_twice, *to_odd, *to_even, *even_twice, *even_once)
    whole = call(
        lambda *refs: combine_body(final, *refs), shape(width + sample_count, width), [VMEM] * 3
    )(cross, message, message_other)
    paired = whole + flipped(whole, 1)
    sums, squares = call(
        lambda *refs: last_solve_body(rounds, final, *refs),
        (shape(1, width), shape(1, width)),
        [VMEM] * 6,
    )(*both_partners(paired), partner, sign)
    return (sums.reshape(width), squares.reshape(width))


def solution(mesh):
    in_specs = (P("rows", "blk"), P("rows", "blk"), P(None, "rows"), P())
    out_specs = (P("blk"), P("blk"))
    return jax.shard_map(
        on_device, mesh=mesh, in_specs=in_specs, out_specs=out_specs, check_vma=False
    )
```

```python
import jax
import jax.numpy as jnp
from jax import lax
from jax.experimental import pallas as pl
from jax.experimental.pallas import tpu as pltpu
from jax.sharding import PartitionSpec as P

f32 = jnp.float32
bf16 = jnp.bfloat16
i32 = jnp.int32
VMEM = pl.BlockSpec(memory_space=pltpu.VMEM)
params = pltpu.CompilerParams(vmem_limit_bytes=24 * 1024 * 1024)
large_params = pltpu.CompilerParams(vmem_limit_bytes=52 * 1024 * 1024)
PIECES = 1


def split(value):
    high = value.astype(bf16)
    low = (value - high.astype(f32)).astype(bf16)
    return high, low


def dot(left, right):
    return jnp.dot(left, right, preferred_element_type=f32)


def dot_rows(left, right):
    return lax.dot_general(left, right, (((0,), (0,)), ((), ())), preferred_element_type=f32)


def dot_fine(left, right):
    return jnp.dot(left, right, precision=lax.Precision.HIGHEST, preferred_element_type=f32)


def rotated(left, right):
    high, low = split(left)
    return dot(jnp.concatenate([high, low, high], 1), right)


def stacked(right):
    high, low = split(right)
    return jnp.concatenate([high, high, low], 0)


def chunks_of(rows, most):
    size = min(rows, most)
    return rows // size, size


def rows_at(index, size):
    return pl.ds(pl.multiple_of(index * size, size), size)


def call(body, out_shape, in_specs):
    return pl.pallas_call(
        body,
        out_shape=out_shape,
        in_specs=in_specs,
        out_specs=jax.tree.map(lambda _: VMEM, out_shape),
        compiler_params=params,
    )


def shape(*dims, dtype=f32):
    return jax.ShapeDtypeStruct(dims, dtype)


def swapped_rows(value):
    half = value.shape[0] // 2
    return jnp.concatenate([value[half:], value[:half]], 0)


def swapped_cols(value):
    half = value.shape[1] // 2
    return jnp.concatenate([value[:, half:], value[:, :half]], 1)


def fetches(source, target, sems, first, cut):
    count, size = chunks_of(target.shape[cut], 1024)
    copies = []
    for i in range(count):
        part = (slice(None),) * cut + (pl.ds(i * size, size),)
        copies.append(pltpu.make_async_copy(source.at[part], target.at[part], sems.at[first + i]))
    return copies, size


def tall(value):
    quarter = value.shape[0] // 2
    return jnp.concatenate([value[:quarter], value[quarter:]], 1)


def square(value):
    half = value.shape[1] // 2
    return jnp.concatenate([value[:, :half], value[:, half:]], 0)


def packed_gram(gram):
    half = gram.shape[0] // 2
    return jnp.concatenate([gram[:half], tall(gram[half:, half:])], 0)


def unpacked_gram(value):
    half = value.shape[1] // 2
    across = value[:half, half:]
    return jnp.concatenate(
        [value[:half], jnp.concatenate([across.T, square(value[half:])], 1)], 0
    )


def first_gram_body(factor_hbm, out_ref, factor_ref, sems):
    width = factor_ref.shape[1]
    copies, size = fetches(factor_hbm, factor_ref, sems, 0, 0)
    for copy in copies:
        copy.start()
    total = jnp.zeros((width, 2 * width), f32)
    for i, copy in enumerate(copies):
        copy.wait()
        high, low = split(factor_ref[i * size : (i + 1) * size, :])
        total += dot_rows(high, jnp.concatenate([high, low], 1))
    cross = total[:, width:]
    out_ref[...] = packed_gram(total[:, :width] + (cross + cross.T))


def first_gram(factor_cols):
    rows, width = factor_cols.shape
    return pl.pallas_call(
        first_gram_body,
        out_shape=shape(width * 3 // 4, width),
        in_specs=[pl.BlockSpec(memory_space=pl.ANY)],
        out_specs=VMEM,
        scratch_shapes=[
            pltpu.VMEM((rows, width), f32),
            pltpu.SemaphoreType.DMA((chunks_of(rows, 1024)[0],)),
        ],
        compiler_params=large_params,
    )(factor_cols)


def project_body(samples_hbm, basis_hbm, order_ref, out_ref, partner_ref, sign_ref, samples_ref, basis_ref, sems):
    width = basis_ref.shape[1]
    lefts, size = fetches(samples_hbm, samples_ref, sems, 0, 1)
    rights, size = fetches(basis_hbm, basis_ref, sems, len(lefts), 0)
    for left, right in zip(lefts, rights):
        left.start()
        right.start()

    lines = order_ref.shape[0]
    order = order_ref[...]
    lane = lax.broadcasted_iota(i32, (lines, width), 1)
    ahead = jnp.concatenate([order[:, 1:], order[:, :1]], 1)
    behind = jnp.concatenate([order[:, -1:], order[:, :-1]], 1)
    even = lane % 2 == 0
    other = jnp.where(even, ahead, behind + width)
    filler = jnp.zeros((width - lines, width), i32)
    order = jnp.concatenate([order, filler], 0).T
    other = jnp.concatenate([other, filler], 0).T
    column = lax.broadcasted_iota(i32, (width, width), 1)
    found = []
    for line in range(lines):
        hits = jnp.where(order[:, line : line + 1] == column, other[:, line : line + 1], 0)
        found.append(jnp.sum(hits, axis=0, keepdims=True))
    found = jnp.concatenate(found, 0)
    first = found < width
    partner_ref[...] = jnp.where(first, found, found - width)
    sign_ref[...] = jnp.where(first, 1.0, -1.0).astype(f32)

    total = jnp.zeros(out_ref.shape, f32)
    for i, (left, right) in enumerate(zip(lefts, rights)):
        left.wait()
        right.wait()
        left_high, left_low = split(samples_ref[:, i * size : (i + 1) * size])
        right_high, right_low = split(basis_ref[i * size : (i + 1) * size, :])
        both = dot(left_high, jnp.concatenate([right_high, right_low], 1))
        total += both[:, :width] + both[:, width:] + dot(left_low, right_high)
    out_ref[...] = total


def project(samples, basis_cols, order):
    rows, width = basis_cols.shape
    lines = order.shape[0]
    return pl.pallas_call(
        project_body,
        out_shape=(
            shape(samples.shape[0], width),
            shape(lines, width, dtype=i32),
            shape(lines, width),
        ),
        in_specs=[pl.BlockSpec(memory_space=pl.ANY)] * 2 + [VMEM],
        out_specs=(VMEM, VMEM, VMEM),
        scratch_shapes=[
            pltpu.VMEM(samples.shape, f32),
            pltpu.VMEM((rows, width), f32),
            pltpu.SemaphoreType.DMA((2 * chunks_of(rows, 1024)[0],)),
        ],
        compiler_params=large_params,
    )(samples, basis_cols, order)


def diagonal_of(value, eye):
    return jnp.sum(jnp.where(eye, value, 0.0), axis=0, keepdims=True)


def lanes(value, index):
    return jnp.take_along_axis(value, index, axis=1, mode="promise_in_bounds")


def eye_of(width):
    row_id = lax.broadcasted_iota(i32, (width, width), 0)
    col_id = lax.broadcasted_iota(i32, (width, width), 1)
    return row_id == col_id


def turn_step(settled, carried, eye, index, sign, last):
    width = settled.shape[0]
    swapped = lanes(settled, index)
    own = diagonal_of(settled, eye)
    crossing = diagonal_of(swapped, eye)
    both = lanes(
        jnp.concatenate([jnp.broadcast_to(own, (8, width)), jnp.broadcast_to(crossing, (8, width))], 0),
        index[:16],
    )
    across = sign * (own - both[0:1])
    up = crossing + both[8:9]
    scale = jnp.maximum(jnp.abs(across), jnp.abs(up))
    found = scale > 0.0
    shrink = 1.0 / jnp.where(found, scale, 1.0)
    level = jnp.where(found, across * shrink, 1.0)
    slope = up * shrink
    inverse = lax.rsqrt(level * level + slope * slope)
    square = 0.5 + 0.5 * jnp.abs(level) * inverse
    against = lax.rsqrt(square)
    major = square * against
    minor = 0.5 * jnp.abs(slope) * inverse * against
    ahead = level >= 0.0
    cosine = jnp.where(ahead, major, minor)
    sine = jnp.where(ahead, minor, major)
    sine = jnp.where(slope < 0.0, -sine, sine) * sign
    carried = carried * cosine + lanes(carried, index) * sine
    if last == "turn":
        return None, carried
    if last == "sums":
        return own * (cosine * cosine) + both[0:1] * (sine * sine) + up * (cosine * sine), carried
    turned = (settled * cosine + swapped * sine).T
    return turned * cosine + lanes(turned, index) * sine, carried


def solve(problems, partners, signs, last=None):
    width = problems[0][0].shape[0]
    eye = eye_of(width)
    for step in range(partners.shape[0]):
        sign = signs[step : step + 1, :]
        index = jnp.broadcast_to(partners[step : step + 1, :], (width, width))
        ending = last if step == partners.shape[0] - 1 else None
        problems = [turn_step(*problem, eye, index, sign, ending) for problem in problems]
    return problems


def round_of(ref, index, rounds):
    steps = ref.shape[0] // rounds
    return ref[index * steps : (index + 1) * steps, :]


def blk_index():
    return lax.axis_index("blk").astype(i32)


def top_goes_odd():
    position = blk_index()
    return jnp.logical_or(position % 2 == 1, position == 0)


def odd_takes_top(final):
    position = blk_index()
    return jnp.logical_or(position % 2 == 0, position == final)


def even_takes_top():
    position = blk_index()
    return jnp.logical_and(position % 2 == 1, position != 1)


def identity_of(width):
    return jnp.where(eye_of(width), 1.0, 0.0).astype(f32)


def first_solve_body(rounds, own_ref, other_ref, partner_ref, sign_ref, turn_ref):
    gram = unpacked_gram(own_ref[...] + other_ref[...])
    ((_, turn_ref[...]),) = solve(
        [(gram, identity_of(gram.shape[0]))],
        round_of(partner_ref, 0, rounds),
        round_of(sign_ref, 0, rounds),
        "turn",
    )


def rotate_body(factor_ref, projected_ref, turn_ref, *out_refs):
    odd_refs, even_refs = out_refs[: len(out_refs) // 2], out_refs[len(out_refs) // 2 :]
    width = factor_ref.shape[1]
    half = width // 2
    packed = factor_ref.shape[0] // 2
    turn = turn_ref[...]
    turn = jnp.where(top_goes_odd(), turn, swapped_cols(turn))
    for_odd, for_even = turn[:, :half], turn[:, half:]
    empty = jnp.zeros_like(for_odd)
    weights = jnp.concatenate(
        [
            jnp.concatenate([for_odd, empty, for_even, empty], 1),
            jnp.concatenate([empty, for_odd, empty, for_even], 1),
        ],
        0,
    )
    weights = stacked(weights)
    piece = packed // len(odd_refs)
    count, size = chunks_of(piece, 512)
    for number, (odd_ref, even_ref) in enumerate(zip(odd_refs, even_refs)):

        def step(i, _):
            start = pl.multiple_of(i * size, size)
            lower = pl.ds(pl.multiple_of(number * piece + start, size), size)
            upper = pl.ds(pl.multiple_of(packed + number * piece + start, size), size)
            left = jnp.concatenate([factor_ref[lower, :], factor_ref[upper, :]], 1)
            result = rotated(left, weights)
            odd_ref[pl.ds(start, size), :] = result[:, :width]
            even_ref[pl.ds(start, size), :] = result[:, width:]
            return 0

        lax.fori_loop(0, count, step, 0)
    extra = projected_ref.shape[0] // 2
    left = jnp.concatenate([projected_ref[:extra, :], projected_ref[extra:, :]], 1)
    result = rotated(left, weights)
    odd_refs[-1][piece : piece + extra, :] = result[:, :width]
    even_refs[-1][piece : piece + extra, :] = result[:, width:]


def folded(whole):
    half = whole.shape[0] // 4

    def block(i, j):
        return whole[i * half : (i + 1) * half, j * half : (j + 1) * half]

    return jnp.concatenate(
        [
            jnp.concatenate([block(0, 0) + block(1, 1), block(0, 2) + block(1, 3)], 1),
            jnp.concatenate([block(2, 0) + block(3, 1), block(2, 2) + block(3, 3)], 1),
        ],
        0,
    )


def second_gram_body(piece, *refs):
    refs, out_ref = refs[:-1], refs[-1]
    odd_refs, even_refs = refs[: len(refs) // 2], refs[len(refs) // 2 :]
    count, size = chunks_of(piece, 512)
    width = 2 * odd_refs[0].shape[1]
    total = jnp.zeros((width, 2 * width), f32)
    for odd_ref, even_ref in zip(odd_refs, even_refs):

        def step(i, total):
            part = rows_at(i, size)
            high, low = split(jnp.concatenate([odd_ref[part, :], even_ref[part, :]], 1))
            return total + dot_rows(high, jnp.concatenate([high, low], 1))

        total = lax.fori_loop(0, count, step, total)
    cross = folded(total[:, width:])
    gram = folded(total[:, :width]) + (cross + cross.T)
    out_ref[...] = packed_gram(jnp.where(blk_index() % 2 == 1, swapped_rows(swapped_cols(gram)), gram))


def second_solve_body(rounds, own_ref, other_ref, partner_ref, sign_ref, odd_ref, even_ref):
    gram = unpacked_gram(own_ref[...] + other_ref[...])
    width = gram.shape[0]
    half = width // 2
    ((settled, turn),) = solve(
        [(gram, identity_of(width))], round_of(partner_ref, 1, rounds), round_of(sign_ref, 1, rounds)
    )
    top = jnp.concatenate([tall(turn[:, :half]), tall(settled[:half, :half])], 0)
    bottom = jnp.concatenate([tall(turn[:, half:]), tall(settled[half:, half:])], 0)
    take_top = top_goes_odd()
    odd_ref[...] = jnp.where(take_top, top, bottom)
    even_ref[...] = jnp.where(take_top, bottom, top)


def cross_body(piece, final, *refs):
    refs, out_ref = refs[:-1], refs[-1]
    number = len(refs) // 5
    odd_far, odd_own, even_own, even_far, even_once = (
        refs[i * number : (i + 1) * number] for i in range(5)
    )
    position = blk_index()
    at_edge = jnp.logical_or(position == 0, position == final)
    width = odd_own[0].shape[1]
    half = width // 2
    count, size = chunks_of(piece, 512)

    def sides(index, part):
        return (
            jnp.concatenate(
                [
                    jnp.where(at_edge, even_once[index][part, :], odd_far[index][part, :]),
                    odd_own[index][part, :],
                ],
                1,
            ),
            jnp.concatenate([even_own[index][part, :], even_far[index][part, :]], 1),
        )

    total = jnp.zeros((2 * width, 2 * width), f32)
    for index in range(number):

        def step(i, total):
            left, right = sides(index, rows_at(i, size))
            left_high, left_low = split(left)
            right_high, right_low = split(right)
            return total + dot_rows(
                jnp.concatenate([left_high, left_high, left_low], 0),
                jnp.concatenate([right_high, right_low, right_high], 0),
            )

        total = lax.fori_loop(0, count, step, total)
    out_ref[:width, :] = folded(total)
    extra = odd_own[-1].shape[0] - piece
    for side, value in enumerate(sides(-1, slice(piece, piece + extra))):
        start = width + side * 2 * extra
        out_ref[start : start + extra, :half] = value[:, :half]
        out_ref[start : start + extra, half:] = value[:, width : width + half]
        out_ref[start + extra : start + 2 * extra, :half] = value[:, half:width]
        out_ref[start + extra : start + 2 * extra, half:] = value[:, width + half :]


def combine_body(final, cross_ref, odd_ref, even_ref, out_ref):
    width = cross_ref.shape[1]
    half = width // 2
    count = (cross_ref.shape[0] - width) // 2
    position = blk_index()
    odd = position % 2 == 1
    at_edge = jnp.logical_or(position == 0, position == final)
    odd_turn, even_turn = square(odd_ref[:half, :]), square(even_ref[:half, :])
    odd_turn = jnp.where(jnp.logical_xor(odd, at_edge), swapped_rows(odd_turn), odd_turn)
    even_turn = jnp.where(odd, swapped_rows(even_turn), even_turn)
    cross = dot_fine(dot_fine(odd_turn.T, cross_ref[:width, :]), even_turn)
    share = 0.25
    odd_gram = square(odd_ref[half:, :]) * share
    even_gram = square(even_ref[half:, :]) * share
    odd_samples = dot_fine(cross_ref[width : width + count, :], odd_turn)
    even_samples = dot_fine(cross_ref[width + count :, :], even_turn)
    first = jnp.where(odd, even_gram, odd_gram)
    second = jnp.where(odd, odd_gram, even_gram)
    cross = jnp.where(odd, cross.T, cross)
    out_ref[:count, :half] = jnp.where(odd, even_samples, odd_samples)
    out_ref[:count, half:] = jnp.where(odd, odd_samples, even_samples)
    out_ref[count : count + half, :half] = first
    out_ref[count : count + half, half:] = cross
    out_ref[count + half :, :] = tall(second)


def last_solve_body(
    rounds, final, odd_ref, odd_other_ref, even_ref, even_other_ref, partner_ref, sign_ref, sums_ref, squares_ref
):
    wholes = [odd_ref[...] + odd_other_ref[...], even_ref[...] + even_other_ref[...]]
    width = wholes[0].shape[1]
    half = width // 2
    samples = wholes[0].shape[0] - width * 3 // 4
    solved = solve(
        [(unpacked_gram(whole[samples:]), whole[:samples]) for whole in wholes],
        round_of(partner_ref, 2, rounds),
        round_of(sign_ref, 2, rounds),
        "sums",
    )
    takes = [odd_takes_top(final), even_takes_top()]
    halves = []
    for (sums, projected), take_top in zip(solved, takes):
        squares = jnp.sum(projected * projected, axis=0, keepdims=True) * (1.0 / samples)
        both = jnp.concatenate([sums, squares], 0)
        halves.append(jnp.where(take_top, both[:, :half], both[:, half:]))
    odd = blk_index() % 2 == 1
    first = jnp.where(odd, halves[1], halves[0])
    second = jnp.where(odd, halves[0], halves[1])
    result = jnp.concatenate([first, second], 1)
    sums_ref[...] = result[0:1]
    squares_ref[...] = result[1:2]


def odd_partner(position, count):
    partner = position - 1 if position % 2 == 0 else position + 1
    return partner if 0 <= partner < count else position


def even_partner(position):
    return position + 1 if position % 2 == 0 else position - 1


def via_odd(value, closed):
    count = lax.axis_size("blk")
    pairs = [(i, odd_partner(i, count)) for i in range(count)]
    return lax.ppermute(value, "blk", [pair for pair in pairs if closed or pair[0] != pair[1]])


def via_even(value):
    count = lax.axis_size("blk")
    return lax.ppermute(value, "blk", [(i, even_partner(i)) for i in range(count)])


def both_chips(value, partner_of):
    count, rows = lax.axis_size("blk"), lax.axis_size("rows")
    pairs = []
    for i in range(count):
        for row in range(rows):
            chip, core = row // 2, row % 2
            pairs.append((i * rows + row, partner_of(i) * rows + core * 2 + chip))
    mine = lax.ppermute(value, ("blk", "rows"), pairs)
    return mine, flipped(mine, 1)


def both_partners(value):
    count = lax.axis_size("blk")
    even = both_chips(value, even_partner)
    odd = both_chips(value, lambda i: odd_partner(i, count))
    return odd + even


def flipped(value, bit):
    return lax.ppermute(value, "rows", [(i, i ^ bit) for i in range(lax.axis_size("rows"))])


def on_device(factor_cols, basis_cols, samples, pairing):
    width = factor_cols.shape[1]
    packed = factor_cols.shape[0] // 2
    sample_count = samples.shape[0]
    extra = sample_count // 2
    rounds, steps = pairing.shape[0], pairing.shape[1]
    piece = packed // PIECES
    final = lax.axis_size("blk") - 1

    gram = first_gram(factor_cols)
    paired = gram + flipped(gram, 1)
    pairing, paired = lax.optimization_barrier((pairing, paired))
    projected, partner, sign = project(samples, basis_cols, pairing.reshape(rounds * steps, width))
    turn = call(lambda *refs: first_solve_body(rounds, *refs), shape(width, width), [VMEM] * 4)(
        paired, flipped(paired, 2), partner, sign
    )
    pieces = [shape(piece + (extra if i == PIECES - 1 else 0), width) for i in range(PIECES)]
    sent = call(rotate_body, tuple(pieces + pieces), [VMEM] * 3)(factor_cols, projected, turn)
    to_odd, to_even = sent[:PIECES], sent[PIECES:]
    odd_once, even_once, odd_twice, even_twice = [], [], [], []
    for i in range(PIECES):
        even_once.append(via_even(to_even[i]))
        odd_once.append(via_odd(to_odd[i], True))
    for i in range(PIECES):
        odd_twice.append(via_odd(even_once[i], False))
        even_twice.append(via_even(odd_once[i]))
    gram = call(lambda *refs: second_gram_body(piece, *refs), shape(width * 3 // 4, width), [VMEM] * (2 * PIECES))(
        *odd_once, *even_once
    )
    paired = gram + flipped(gram, 1)
    for_odd, for_even = call(
        lambda *refs: second_solve_body(rounds, *refs),
        (shape(width * 3 // 4, width), shape(width * 3 // 4, width)),
        [VMEM] * 4,
    )(paired, flipped(paired, 2), partner, sign)
    from_even = via_even(for_even)
    from_odd = via_odd(for_odd, True)
    cross = call(
        lambda *refs: cross_body(piece, final, *refs),
        shape(width + 2 * sample_count, width),
        [VMEM] * (5 * PIECES),
    )(*odd_twice, *to_odd, *to_even, *even_twice, *even_once)
    whole = call(
        lambda *refs: combine_body(final, *refs), shape(width * 3 // 4 + sample_count, width), [VMEM] * 3
    )(cross, from_odd, from_even)
    paired = whole + flipped(whole, 1)
    sums, squares = call(
        lambda *refs: last_solve_body(rounds, final, *refs),
        (shape(1, width), shape(1, width)),
        [VMEM] * 6,
    )(*both_partners(paired), partner, sign)
    return (sums.reshape(width), squares.reshape(width))


def solution(mesh):
    in_specs = (P("rows", "blk"), P("rows", "blk"), P(None, "rows"), P())
    out_specs = (P("blk"), P("blk"))
    return jax.shard_map(
        on_device, mesh=mesh, in_specs=in_specs, out_specs=out_specs, check_vma=False
    )
```

```python
import jax
import jax.numpy as jnp
from jax import lax
from jax.experimental import pallas as pl
from jax.experimental.pallas import tpu as pltpu
from jax.sharding import PartitionSpec as P

f32 = jnp.float32
bf16 = jnp.bfloat16
i32 = jnp.int32
VMEM = pl.BlockSpec(memory_space=pltpu.VMEM)
params = pltpu.CompilerParams(vmem_limit_bytes=24 * 1024 * 1024)
CHUNKS = 8
CUT = 5
large_params = pltpu.CompilerParams(vmem_limit_bytes=52 * 1024 * 1024)


def split(value):
    high = value.astype(bf16)
    low = (value - high.astype(f32)).astype(bf16)
    return high, low


def dot(left, right):
    return jnp.dot(left, right, preferred_element_type=f32)


def dot_rows(left, right):
    return lax.dot_general(left, right, (((0,), (0,)), ((), ())), preferred_element_type=f32)


def rotated(left, right):
    high, low = split(left)
    return dot(jnp.concatenate([high, low, high], 1), right)


def stacked(right):
    high, low = split(right)
    return jnp.concatenate([high, high, low], 0)


def chunks_of(rows, most):
    size = min(rows, most)
    return rows // size, size


def part(refs, start, size):
    for ref in refs:
        if start < ref.shape[0]:
            return ref[start : start + size, :]
        start -= ref.shape[0]


def put(refs, start, value):
    for ref in refs:
        if start < ref.shape[0]:
            ref[start : start + value.shape[0], :] = value
            return
        start -= ref.shape[0]


def call(body, out_shape, in_specs):
    return pl.pallas_call(
        body,
        out_shape=out_shape,
        in_specs=in_specs,
        out_specs=jax.tree.map(lambda _: VMEM, out_shape),
        compiler_params=params,
        cost_estimate=pl.CostEstimate(flops=1, bytes_accessed=1, transcendentals=0),
    )


def shape(*dims, dtype=f32):
    return jax.ShapeDtypeStruct(dims, dtype)


def swapped_rows(value):
    half = value.shape[0] // 2
    return jnp.concatenate([value[half:], value[:half]], 0)


def swapped_cols(value):
    half = value.shape[1] // 2
    return jnp.concatenate([value[:, half:], value[:, :half]], 1)


def fetches(source, target, sems, first, cut):
    count, size = chunks_of(target.shape[cut], 1024)
    copies = []
    for i in range(count):
        part = (slice(None),) * cut + (pl.ds(i * size, size),)
        copies.append(pltpu.make_async_copy(source.at[part], target.at[part], sems.at[first + i]))
    return copies, size


def tall(value):
    quarter = value.shape[0] // 2
    return jnp.concatenate([value[:quarter], value[quarter:]], 1)


def square(value):
    half = value.shape[1] // 2
    return jnp.concatenate([value[:, :half], value[:, half:]], 0)


def packed_gram(gram):
    half = gram.shape[0] // 2
    return jnp.concatenate([gram[:half], tall(gram[half:, half:])], 0)


def unpacked_gram(value):
    half = value.shape[1] // 2
    across = value[:half, half:]
    return jnp.concatenate(
        [value[:half], jnp.concatenate([across.T, square(value[half:])], 1)], 0
    )


def first_gram_body(factor_hbm, out_ref, factor_ref, sems):
    width = factor_ref.shape[1]
    copies, size = fetches(factor_hbm, factor_ref, sems, 0, 0)
    for copy in copies:
        copy.start()
    total = jnp.zeros((width, 2 * width), f32)
    for i, copy in enumerate(copies):
        copy.wait()
        high, low = split(factor_ref[i * size : (i + 1) * size, :])
        total += dot_rows(high, jnp.concatenate([high, low], 1))
    cross = total[:, width:]
    out_ref[...] = packed_gram(total[:, :width] + (cross + cross.T))


def first_gram(factor_cols):
    rows, width = factor_cols.shape
    return pl.pallas_call(
        first_gram_body,
        out_shape=shape(width * 3 // 4, width),
        in_specs=[pl.BlockSpec(memory_space=pl.ANY)],
        out_specs=VMEM,
        scratch_shapes=[
            pltpu.VMEM((rows, width), f32),
            pltpu.SemaphoreType.DMA((chunks_of(rows, 1024)[0],)),
        ],
        compiler_params=large_params,
    )(factor_cols)


def project_body(samples_hbm, basis_hbm, order_ref, out_ref, partner_ref, sign_ref, samples_ref, basis_ref, sems):
    width = basis_ref.shape[1]
    lefts, size = fetches(samples_hbm, samples_ref, sems, 0, 1)
    rights, size = fetches(basis_hbm, basis_ref, sems, len(lefts), 0)
    for left, right in zip(lefts, rights):
        left.start()
        right.start()

    lines = order_ref.shape[0]
    order = order_ref[...]
    lane = lax.broadcasted_iota(i32, (lines, width), 1)
    ahead = jnp.concatenate([order[:, 1:], order[:, :1]], 1)
    behind = jnp.concatenate([order[:, -1:], order[:, :-1]], 1)
    even = lane % 2 == 0
    other = jnp.where(even, ahead, behind + width)
    filler = jnp.zeros((width - lines, width), i32)
    order = jnp.concatenate([order, filler], 0).T
    other = jnp.concatenate([other, filler], 0).T
    column = lax.broadcasted_iota(i32, (width, width), 1)
    found = []
    for line in range(lines):
        hits = jnp.where(order[:, line : line + 1] == column, other[:, line : line + 1], 0)
        found.append(jnp.sum(hits, axis=0, keepdims=True))
    found = jnp.concatenate(found, 0)
    first = found < width
    partner_ref[...] = jnp.where(first, found, found - width)
    sign_ref[...] = jnp.where(first, 1.0, -1.0).astype(f32)

    total = jnp.zeros(out_ref.shape, f32)
    for i, (left, right) in enumerate(zip(lefts, rights)):
        left.wait()
        right.wait()
        left_high, left_low = split(samples_ref[:, i * size : (i + 1) * size])
        right_high, right_low = split(basis_ref[i * size : (i + 1) * size, :])
        both = dot(left_high, jnp.concatenate([right_high, right_low], 1))
        total += both[:, :width] + both[:, width:] + dot(left_low, right_high)
    out_ref[...] = total


def project(samples, basis_cols, order):
    rows, width = basis_cols.shape
    lines = order.shape[0]
    return pl.pallas_call(
        project_body,
        out_shape=(
            shape(samples.shape[0], width),
            shape(lines, width, dtype=i32),
            shape(lines, width),
        ),
        in_specs=[pl.BlockSpec(memory_space=pl.ANY)] * 2 + [VMEM],
        out_specs=(VMEM, VMEM, VMEM),
        scratch_shapes=[
            pltpu.VMEM(samples.shape, f32),
            pltpu.VMEM((rows, width), f32),
            pltpu.SemaphoreType.DMA((2 * chunks_of(rows, 1024)[0],)),
        ],
        compiler_params=large_params,
    )(samples, basis_cols, order)


def lanes(value, index):
    return jnp.take_along_axis(value, index, axis=1, mode="promise_in_bounds")


def eye_of(width):
    row_id = lax.broadcasted_iota(i32, (width, width), 0)
    col_id = lax.broadcasted_iota(i32, (width, width), 1)
    return row_id == col_id


def column_sums(value):
    total = jnp.sum(value.reshape(-1, 8, value.shape[1]), axis=0)
    for shift in (4, 2, 1):
        total += pltpu.roll(total, shift, 0)
    return total


def scaled(value, factor):
    return (value.reshape(-1, 8, value.shape[1]) * factor[None]).reshape(value.shape)


def turn_step(settled, carried, eye, index, facing, sign, last):
    swapped = lanes(settled, index)
    own = column_sums(jnp.where(eye, settled, 0.0))
    other = column_sums(jnp.where(facing, swapped, 0.0))
    up = column_sums(jnp.where(eye, swapped, 0.0)) + column_sums(jnp.where(facing, settled, 0.0))
    across = sign * (own - other)
    scale = jnp.maximum(jnp.abs(across), jnp.abs(up))
    found = scale > 0.0
    shrink = 1.0 / jnp.where(found, scale, 1.0)
    level = jnp.where(found, across * shrink, 1.0)
    slope = up * shrink
    inverse = lax.rsqrt(level * level + slope * slope)
    major_square = 0.5 + 0.5 * jnp.abs(level) * inverse
    against = lax.rsqrt(major_square)
    major = major_square * against
    minor = 0.5 * jnp.abs(slope) * inverse * against
    ahead = level >= 0.0
    cosine = jnp.where(ahead, major, minor)
    sine = jnp.where(ahead, minor, major)
    sine = jnp.where(slope < 0.0, -sine, sine) * sign
    carried = scaled(carried, cosine) + scaled(lanes(carried, index), sine)
    if last == "turn":
        return None, carried
    if last == "sums":
        sums = own * (cosine * cosine) + other * (sine * sine) + up * (cosine * sine)
        return sums[0:1], carried
    turned = (scaled(settled, cosine) + scaled(swapped, sine)).T
    return scaled(turned, cosine) + scaled(lanes(turned, index), sine), carried


def solve(problems, partners, signs, last=None):
    width = problems[0][0].shape[0]
    eye = eye_of(width)
    row_id = lax.broadcasted_iota(i32, (width, width), 0)
    for step in range(partners.shape[0]):
        sign = jnp.broadcast_to(signs[step : step + 1, :], (8, width))
        index = jnp.broadcast_to(partners[step : step + 1, :], (width, width))
        ending = last if step == partners.shape[0] - 1 else None
        problems = [turn_step(*problem, eye, index, row_id == index, sign, ending) for problem in problems]
    return problems


def round_of(ref, index, rounds):
    steps = ref.shape[0] // rounds
    return ref[index * steps : (index + 1) * steps, :]


def blk_index():
    return lax.axis_index("blk").astype(i32)


def top_goes_odd():
    position = blk_index()
    return jnp.logical_or(position % 2 == 1, position == 0)


def odd_takes_top(final):
    position = blk_index()
    return jnp.logical_or(position % 2 == 0, position == final)


def even_takes_top():
    position = blk_index()
    return jnp.logical_and(position % 2 == 1, position != 1)


def identity_of(width):
    return jnp.where(eye_of(width), 1.0, 0.0).astype(f32)


def first_solve_body(rounds, own_ref, other_ref, partner_ref, sign_ref, turn_ref):
    gram = unpacked_gram(own_ref[...] + other_ref[...])
    ((_, turn_ref[...]),) = solve(
        [(gram, identity_of(gram.shape[0]))],
        round_of(partner_ref, 0, rounds),
        round_of(sign_ref, 0, rounds),
        "turn",
    )


def rotate_body(odd_count, factor_ref, projected_ref, turn_ref, *out_refs):
    odd_refs, even_refs = out_refs[:odd_count], out_refs[odd_count:]
    width = factor_ref.shape[1]
    half = width // 2
    packed = factor_ref.shape[0] // 2
    turn = turn_ref[...]
    turn = jnp.where(top_goes_odd(), turn, swapped_cols(turn))
    for_odd, for_even = turn[:, :half], turn[:, half:]
    empty = jnp.zeros_like(for_odd)
    weights = jnp.concatenate(
        [
            jnp.concatenate([for_odd, empty, for_even, empty], 1),
            jnp.concatenate([empty, for_odd, empty, for_even], 1),
        ],
        0,
    )
    weights = stacked(weights)

    def spread(start, lower, upper):
        result = rotated(jnp.concatenate([lower, upper], 1), weights)
        put(odd_refs, start, result[:, :width])
        put(even_refs, start, result[:, width:])

    size = packed // CHUNKS
    for start in range(0, packed, size):
        spread(start, factor_ref[start : start + size, :], factor_ref[packed + start : packed + start + size, :])
    extra = projected_ref.shape[0] // 2
    spread(packed, projected_ref[:extra, :], projected_ref[extra:, :])


def folded(whole):
    half = whole.shape[0] // 4

    def block(i, j):
        return whole[i * half : (i + 1) * half, j * half : (j + 1) * half]

    return jnp.concatenate(
        [
            jnp.concatenate([block(0, 0) + block(1, 1), block(0, 2) + block(1, 3)], 1),
            jnp.concatenate([block(2, 0) + block(3, 1), block(2, 2) + block(3, 3)], 1),
        ],
        0,
    )


def second_gram_body(packed, count, *refs):
    refs, out_ref = refs[:-1], refs[-1]
    odd_refs, even_refs = refs[:count], refs[count:]
    size = packed // CHUNKS
    width = 2 * refs[0].shape[1]
    total = jnp.zeros((width, 2 * width), f32)
    for start in range(0, packed, size):
        high, low = split(
            jnp.concatenate([part(odd_refs, start, size), part(even_refs, start, size)], 1)
        )
        total += dot_rows(high, jnp.concatenate([high, low], 1))
    cross = folded(total[:, width:])
    gram = folded(total[:, :width]) + (cross + cross.T)
    gram = jnp.where(blk_index() % 2 == 1, swapped_rows(swapped_cols(gram)), gram)
    out_ref[...] = packed_gram(gram)


def second_solve_body(rounds, own_ref, other_ref, partner_ref, sign_ref, odd_ref, even_ref):
    gram = unpacked_gram(own_ref[...] + other_ref[...])
    width = gram.shape[0]
    half = width // 2
    ((settled, turn),) = solve(
        [(gram, identity_of(width))], round_of(partner_ref, 1, rounds), round_of(sign_ref, 1, rounds)
    )
    top = jnp.concatenate([tall(turn[:, :half]), tall(settled[:half, :half])], 0)
    bottom = jnp.concatenate([tall(turn[:, half:]), tall(settled[half:, half:])], 0)
    take_top = top_goes_odd()
    odd_ref[...] = jnp.where(take_top, top, bottom)
    even_ref[...] = jnp.where(take_top, bottom, top)


def cross_body(packed, extra, final, odd_far, odd_own, even_own, even_far, even_once, *refs):
    before_refs, out_ref = refs[:-1], refs[-1]
    width = odd_own.shape[1]
    half = width // 2
    position = blk_index()
    at_edge = jnp.logical_or(position == 0, position == final)

    def sides(start, end):
        odd_side = jnp.where(at_edge, even_once[start:end, :], odd_far[start:end, :])
        return (
            jnp.concatenate([odd_side, odd_own[start:end, :]], 1),
            jnp.concatenate([even_own[start:end, :], even_far[start:end, :]], 1),
        )

    size = packed // CHUNKS
    rows = odd_own.shape[0] - extra
    total = jnp.zeros((2 * width, 2 * width), f32)
    for start in range(0, rows, size):
        left, right = sides(start, start + size)
        left_high, left_low = split(left)
        right_high, right_low = split(right)
        total += dot_rows(
            jnp.concatenate([left_high, left_high, left_low], 0),
            jnp.concatenate([right_high, right_low, right_high], 0),
        )
    total = folded(total)
    for ref in before_refs:
        total += ref[...]
    out_ref[:width, :] = total
    if extra:
        for side, value in enumerate(sides(rows, rows + extra)):
            start = width + side * 2 * extra
            out_ref[start : start + extra, :half] = value[:, :half]
            out_ref[start : start + extra, half:] = value[:, width : width + half]
            out_ref[start + extra : start + 2 * extra, :half] = value[:, half:width]
            out_ref[start + extra : start + 2 * extra, half:] = value[:, width + half :]


def combine_body(final, cross_ref, odd_ref, even_ref, out_ref):
    width = cross_ref.shape[1]
    half = width // 2
    count = (cross_ref.shape[0] - width) // 2
    position = blk_index()
    odd = position % 2 == 1
    at_edge = jnp.logical_or(position == 0, position == final)
    odd_turn, even_turn = square(odd_ref[:half, :]), square(even_ref[:half, :])
    odd_turn = jnp.where(jnp.logical_xor(odd, at_edge), swapped_rows(odd_turn), odd_turn)
    even_turn = jnp.where(odd, swapped_rows(even_turn), even_turn)
    odd_stack, even_stack = stacked(odd_turn), stacked(even_turn)
    high, low = split(rotated(cross_ref[:width, :], even_stack))
    cross = dot_rows(odd_stack, jnp.concatenate([high, low, high], 0))
    share = 0.25
    odd_gram = square(odd_ref[half:, :]) * share
    even_gram = square(even_ref[half:, :]) * share
    odd_samples = rotated(cross_ref[width : width + count, :], odd_stack)
    even_samples = rotated(cross_ref[width + count :, :], even_stack)
    first = jnp.where(odd, even_gram, odd_gram)
    second = jnp.where(odd, odd_gram, even_gram)
    cross = jnp.where(odd, cross.T, cross)
    out_ref[:count, :half] = jnp.where(odd, even_samples, odd_samples)
    out_ref[:count, half:] = jnp.where(odd, odd_samples, even_samples)
    out_ref[count : count + half, :half] = first
    out_ref[count : count + half, half:] = cross
    out_ref[count + half : count + half + half // 2, :] = tall(second)
    out_ref[count + half + half // 2 :, :] = jnp.zeros((8, width), f32)


def last_solve_body(
    rounds, final, odd_ref, odd_other_ref, even_ref, even_other_ref, partner_ref, sign_ref, sums_ref, squares_ref
):
    kept = odd_ref.shape[0]
    wholes = [odd_ref[...] + odd_other_ref[...], even_ref[:kept, :] + even_other_ref[:kept, :]]
    width = wholes[0].shape[1]
    half = width // 2
    samples = wholes[0].shape[0] - width * 3 // 4
    solved = solve(
        [(unpacked_gram(whole[samples:]), whole[:samples]) for whole in wholes],
        round_of(partner_ref, 2, rounds),
        round_of(sign_ref, 2, rounds),
        "sums",
    )
    takes = [odd_takes_top(final), even_takes_top()]
    halves = []
    for (sums, projected), take_top in zip(solved, takes):
        squares = jnp.sum(projected * projected, axis=0, keepdims=True) * (1.0 / samples)
        both = jnp.concatenate([sums, squares], 0)
        halves.append(jnp.where(take_top, both[:, :half], both[:, half:]))
    odd = blk_index() % 2 == 1
    first = jnp.where(odd, halves[1], halves[0])
    second = jnp.where(odd, halves[0], halves[1])
    result = jnp.concatenate([first, second], 1)
    sums_ref[...] = result[0:1]
    squares_ref[...] = result[1:2]


def odd_partner(position, count):
    partner = position - 1 if position % 2 == 0 else position + 1
    return partner if 0 <= partner < count else position


def even_partner(position):
    return position + 1 if position % 2 == 0 else position - 1


def via_odd(value, closed):
    count = lax.axis_size("blk")
    pairs = [(i, odd_partner(i, count)) for i in range(count)]
    return lax.ppermute(value, "blk", [pair for pair in pairs if closed or pair[0] != pair[1]])


def via_even(value):
    count = lax.axis_size("blk")
    return lax.ppermute(value, "blk", [(i, even_partner(i)) for i in range(count)])


def both_chips(value, partner_of):
    count, rows = lax.axis_size("blk"), lax.axis_size("rows")
    pairs = []
    for i in range(count):
        for row in range(rows):
            chip, core = row // 2, row % 2
            pairs.append((i * rows + row, partner_of(i) * rows + core * 2 + chip))
    mine = lax.ppermute(value, ("blk", "rows"), pairs)
    return mine, flipped(mine, 1)


def both_partners(value):
    count = lax.axis_size("blk")
    even = both_chips(value, even_partner)
    odd = both_chips(value[:-8], lambda i: odd_partner(i, count))
    return odd + even


def flipped(value, bit):
    return lax.ppermute(value, "rows", [(i, i ^ bit) for i in range(lax.axis_size("rows"))])


def on_device(factor_cols, basis_cols, samples, pairing):
    width = factor_cols.shape[1]
    packed = factor_cols.shape[0] // 2
    sample_count = samples.shape[0]
    extra = sample_count // 2
    rounds, steps = pairing.shape[0], pairing.shape[1]
    final = lax.axis_size("blk") - 1

    gram = first_gram(factor_cols)
    paired = gram + flipped(gram, 1)
    pairing, paired = lax.optimization_barrier((pairing, paired))
    projected, partner, sign = project(samples, basis_cols, pairing.reshape(rounds * steps, width))
    turn = call(lambda *refs: first_solve_body(rounds, *refs), shape(width, width), [VMEM] * 4)(
        paired, flipped(paired, 2), partner, sign
    )
    first, second = packed * CUT // CHUNKS, packed * (CHUNKS - CUT) // CHUNKS + extra
    pieces = [shape(first, width), shape(second, width)]
    count = len(pieces)
    sent = call(
        lambda *refs: rotate_body(count, *refs), tuple(pieces + pieces), [VMEM] * 3
    )(factor_cols, projected, turn)
    to_odd, to_even = sent[:count], sent[count:]
    even_once = [via_even(value) for value in to_even]
    odd_once = [via_odd(value, True) for value in to_odd]
    odd_twice = [via_odd(value, False) for value in even_once]
    even_twice = [via_even(value) for value in odd_once]
    gram = call(
        lambda *refs: second_gram_body(packed, count, *refs),
        shape(width * 3 // 4, width),
        [VMEM] * (2 * count),
    )(*odd_once, *even_once)
    paired = gram + flipped(gram, 1)
    for_odd, for_even = call(
        lambda *refs: second_solve_body(rounds, *refs),
        (shape(width * 3 // 4, width), shape(width * 3 // 4, width)),
        [VMEM] * 4,
    )(paired, flipped(paired, 2), partner, sign)
    groups = [list(group) for group in zip(odd_twice, to_odd, to_even, even_twice, even_once)]
    groups[0][1], for_odd, for_even = lax.optimization_barrier((groups[0][1], for_odd, for_even))
    cross = call(lambda *refs: cross_body(packed, 0, final, *refs), shape(width, width), [VMEM] * 5)(*groups[0])
    from_even = via_even(for_even)
    from_odd = via_odd(for_odd, True)
    cross = call(
        lambda *refs: cross_body(packed, extra, final, *refs), shape(width + 2 * sample_count, width), [VMEM] * 6
    )(*groups[1], cross)
    whole = call(
        lambda *refs: combine_body(final, *refs), shape(width * 3 // 4 + sample_count + 8, width), [VMEM] * 3
    )(cross, from_odd, from_even)
    paired = whole + flipped(whole, 1)
    sums, squares = call(
        lambda *refs: last_solve_body(rounds, final, *refs),
        (shape(1, width), shape(1, width)),
        [VMEM] * 6,
    )(*both_partners(paired), partner, sign)
    return (sums.reshape(width), squares.reshape(width))


def solution(mesh):
    in_specs = (P("rows", "blk"), P("rows", "blk"), P(None, "rows"), P())
    out_specs = (P("blk"), P("blk"))
    return jax.shard_map(
        on_device, mesh=mesh, in_specs=in_specs, out_specs=out_specs, check_vma=False
    )
```

```python
import jax
import jax.numpy as jnp
from jax import lax
from jax.experimental import pallas as pl
from jax.experimental.pallas import tpu as pltpu
from jax.sharding import PartitionSpec as P

f32 = jnp.float32
bf16 = jnp.bfloat16
i32 = jnp.int32
VMEM = pl.BlockSpec(memory_space=pltpu.VMEM)
params = pltpu.CompilerParams(vmem_limit_bytes=24 * 1024 * 1024)
CHUNKS = 8
CUT = 5
large_params = pltpu.CompilerParams(vmem_limit_bytes=52 * 1024 * 1024)


def split(value):
    high = value.astype(bf16)
    low = (value - high.astype(f32)).astype(bf16)
    return high, low


def dot(left, right):
    return jnp.dot(left, right, preferred_element_type=f32)


def dot_rows(left, right):
    return lax.dot_general(left, right, (((0,), (0,)), ((), ())), preferred_element_type=f32)


def rotated(left, right):
    high, low = split(left)
    return dot(jnp.concatenate([high, low, high], 1), right)


def stacked(right):
    high, low = split(right)
    return jnp.concatenate([high, high, low], 0)


def chunks_of(rows, most):
    size = min(rows, most)
    return rows // size, size


def part(refs, start, size):
    for ref in refs:
        if start < ref.shape[0]:
            return ref[start : start + size, :]
        start -= ref.shape[0]


def put(refs, start, value):
    for ref in refs:
        if start < ref.shape[0]:
            ref[start : start + value.shape[0], :] = value
            return
        start -= ref.shape[0]


def call(body, out_shape, in_specs, work=1):
    return pl.pallas_call(
        body,
        out_shape=out_shape,
        in_specs=in_specs,
        out_specs=jax.tree.map(lambda _: VMEM, out_shape),
        compiler_params=params,
        cost_estimate=pl.CostEstimate(flops=work, bytes_accessed=1, transcendentals=0),
    )


def shape(*dims, dtype=f32):
    return jax.ShapeDtypeStruct(dims, dtype)


def swapped_rows(value):
    half = value.shape[0] // 2
    return jnp.concatenate([value[half:], value[:half]], 0)


def swapped_cols(value):
    half = value.shape[1] // 2
    return jnp.concatenate([value[:, half:], value[:, :half]], 1)


def fetches(source, target, sems, first, cut):
    count, size = chunks_of(target.shape[cut], 1024)
    copies = []
    for i in range(count):
        part = (slice(None),) * cut + (pl.ds(i * size, size),)
        copies.append(pltpu.make_async_copy(source.at[part], target.at[part], sems.at[first + i]))
    return copies, size


def tall(value):
    quarter = value.shape[0] // 2
    return jnp.concatenate([value[:quarter], value[quarter:]], 1)


def square(value):
    half = value.shape[1] // 2
    return jnp.concatenate([value[:, :half], value[:, half:]], 0)


def packed_gram(gram):
    half = gram.shape[0] // 2
    return jnp.concatenate([gram[:half], tall(gram[half:, half:])], 0)


def unpacked_gram(value):
    half = value.shape[1] // 2
    across = value[:half, half:]
    return jnp.concatenate(
        [value[:half], jnp.concatenate([across.T, square(value[half:])], 1)], 0
    )


def first_gram_body(factor_hbm, out_ref, factor_ref, sems):
    width = factor_ref.shape[1]
    copies, size = fetches(factor_hbm, factor_ref, sems, 0, 0)
    for copy in copies:
        copy.start()
    total = jnp.zeros((width, 2 * width), f32)
    for i, copy in enumerate(copies):
        copy.wait()
        high, low = split(factor_ref[i * size : (i + 1) * size, :])
        total += dot_rows(high, jnp.concatenate([high, low], 1))
    cross = total[:, width:]
    out_ref[...] = packed_gram(total[:, :width] + (cross + cross.T))


def first_gram(factor_cols):
    rows, width = factor_cols.shape
    return pl.pallas_call(
        first_gram_body,
        out_shape=shape(width * 3 // 4, width),
        in_specs=[pl.BlockSpec(memory_space=pl.ANY)],
        out_specs=VMEM,
        scratch_shapes=[
            pltpu.VMEM((rows, width), f32),
            pltpu.SemaphoreType.DMA((chunks_of(rows, 1024)[0],)),
        ],
        compiler_params=large_params,
    )(factor_cols)


def project_body(samples_hbm, basis_hbm, order_ref, mine_ref, theirs_ref, partner_ref, sign_ref, samples_ref, basis_ref, sems):
    width = basis_ref.shape[1]
    lefts, size = fetches(samples_hbm, samples_ref, sems, 0, 1)
    rights, size = fetches(basis_hbm, basis_ref, sems, len(lefts), 0)
    for left, right in zip(lefts, rights):
        left.start()
        right.start()

    lines = order_ref.shape[0]
    order = order_ref[...]
    lane = lax.broadcasted_iota(i32, (lines, width), 1)
    ahead = jnp.concatenate([order[:, 1:], order[:, :1]], 1)
    behind = jnp.concatenate([order[:, -1:], order[:, :-1]], 1)
    even = lane % 2 == 0
    other = jnp.where(even, ahead, behind + width)
    filler = jnp.zeros((width - lines, width), i32)
    order = jnp.concatenate([order, filler], 0).T
    other = jnp.concatenate([other, filler], 0).T
    column = lax.broadcasted_iota(i32, (width, width), 1)
    found = []
    for line in range(lines):
        hits = jnp.where(order[:, line : line + 1] == column, other[:, line : line + 1], 0)
        found.append(jnp.sum(hits, axis=0, keepdims=True))
    found = jnp.concatenate(found, 0)
    first = found < width
    partner_ref[...] = jnp.where(first, found, found - width)
    sign_ref[...] = jnp.where(first, 1.0, -1.0).astype(f32)

    total = jnp.zeros((samples_ref.shape[0], width), f32)
    for i, (left, right) in enumerate(zip(lefts, rights)):
        left.wait()
        right.wait()
        left_high, left_low = split(samples_ref[:, i * size : (i + 1) * size])
        right_high, right_low = split(basis_ref[i * size : (i + 1) * size, :])
        both = dot(left_high, jnp.concatenate([right_high, right_low], 1))
        total += both[:, :width] + both[:, width:] + dot(left_low, right_high)
    half = total.shape[0] // 2
    first_core = lax.axis_index("rows") % 2 == 0
    mine_ref[...] = jnp.where(first_core, total[:half], total[half:])
    theirs_ref[...] = jnp.where(first_core, total[half:], total[:half])


def project(samples, basis_cols, order):
    rows, width = basis_cols.shape
    lines = order.shape[0]
    return pl.pallas_call(
        project_body,
        out_shape=(
            shape(samples.shape[0] // 2, width),
            shape(samples.shape[0] // 2, width),
            shape(lines, width, dtype=i32),
            shape(lines, width),
        ),
        in_specs=[pl.BlockSpec(memory_space=pl.ANY)] * 2 + [VMEM],
        out_specs=(VMEM, VMEM, VMEM, VMEM),
        scratch_shapes=[
            pltpu.VMEM(samples.shape, f32),
            pltpu.VMEM((rows, width), f32),
            pltpu.SemaphoreType.DMA((2 * chunks_of(rows, 1024)[0],)),
        ],
        compiler_params=large_params,
    )(samples, basis_cols, order)


def lanes(value, index):
    return jnp.take_along_axis(value, index, axis=1, mode="promise_in_bounds")


def eye_of(width):
    row_id = lax.broadcasted_iota(i32, (width, width), 0)
    col_id = lax.broadcasted_iota(i32, (width, width), 1)
    return row_id == col_id


def column_sums(value):
    total = jnp.sum(value.reshape(-1, 8, value.shape[1]), axis=0)
    for shift in (4, 2, 1):
        total += pltpu.roll(total, shift, 0)
    return total


def scaled(value, factor):
    return (value.reshape(-1, 8, value.shape[1]) * factor[None]).reshape(value.shape)


def turn_step(settled, carried, eye, index, facing, sign, last):
    swapped = lanes(settled, index)
    own = column_sums(jnp.where(eye, settled, 0.0))
    other = column_sums(jnp.where(facing, swapped, 0.0))
    up = column_sums(jnp.where(eye, swapped, 0.0)) + column_sums(jnp.where(facing, settled, 0.0))
    across = sign * (own - other)
    scale = jnp.maximum(jnp.abs(across), jnp.abs(up))
    found = scale > 0.0
    shrink = 1.0 / jnp.where(found, scale, 1.0)
    level = jnp.where(found, across * shrink, 1.0)
    slope = up * shrink
    inverse = lax.rsqrt(level * level + slope * slope)
    major_square = 0.5 + 0.5 * jnp.abs(level) * inverse
    against = lax.rsqrt(major_square)
    major = major_square * against
    minor = 0.5 * jnp.abs(slope) * inverse * against
    ahead = level >= 0.0
    cosine = jnp.where(ahead, major, minor)
    sine = jnp.where(ahead, minor, major)
    sine = jnp.where(slope < 0.0, -sine, sine) * sign
    carried = scaled(carried, cosine) + scaled(lanes(carried, index), sine)
    if last == "turn":
        return None, carried
    if last == "sums":
        sums = own * (cosine * cosine) + other * (sine * sine) + up * (cosine * sine)
        return sums[0:1], carried
    turned = (scaled(settled, cosine) + scaled(swapped, sine)).T
    return scaled(turned, cosine) + scaled(lanes(turned, index), sine), carried


def solve(problems, partners, signs, last=None):
    width = problems[0][0].shape[0]
    eye = eye_of(width)
    row_id = lax.broadcasted_iota(i32, (width, width), 0)
    for step in range(partners.shape[0]):
        sign = jnp.broadcast_to(signs[step : step + 1, :], (8, width))
        index = jnp.broadcast_to(partners[step : step + 1, :], (width, width))
        ending = last if step == partners.shape[0] - 1 else None
        problems = [turn_step(*problem, eye, index, row_id == index, sign, ending) for problem in problems]
    return problems


def round_of(ref, index, rounds):
    steps = ref.shape[0] // rounds
    return ref[index * steps : (index + 1) * steps, :]


def blk_index():
    return lax.axis_index("blk").astype(i32)


def top_goes_odd():
    position = blk_index()
    return jnp.logical_or(position % 2 == 1, position == 0)


def odd_takes_top(final):
    position = blk_index()
    return jnp.logical_or(position % 2 == 0, position == final)


def even_takes_top():
    position = blk_index()
    return jnp.logical_and(position % 2 == 1, position != 1)


def identity_of(width):
    return jnp.where(eye_of(width), 1.0, 0.0).astype(f32)


def first_solve_body(rounds, own_ref, other_ref, partner_ref, sign_ref, turn_ref):
    gram = unpacked_gram(own_ref[...] + other_ref[...])
    ((_, turn_ref[...]),) = solve(
        [(gram, identity_of(gram.shape[0]))],
        round_of(partner_ref, 0, rounds),
        round_of(sign_ref, 0, rounds),
        "turn",
    )


def rotate_body(odd_count, factor_ref, projected_ref, turn_ref, *out_refs):
    odd_refs, even_refs = out_refs[:odd_count], out_refs[odd_count:]
    width = factor_ref.shape[1]
    half = width // 2
    packed = factor_ref.shape[0] // 2
    turn = turn_ref[...]
    turn = jnp.where(top_goes_odd(), turn, swapped_cols(turn))
    for_odd, for_even = turn[:, :half], turn[:, half:]
    empty = jnp.zeros_like(for_odd)
    weights = jnp.concatenate(
        [
            jnp.concatenate([for_odd, empty, for_even, empty], 1),
            jnp.concatenate([empty, for_odd, empty, for_even], 1),
        ],
        0,
    )
    weights = stacked(weights)

    def spread(start, lower, upper):
        result = rotated(jnp.concatenate([lower, upper], 1), weights)
        put(odd_refs, start, result[:, :width])
        put(even_refs, start, result[:, width:])

    size = packed // CHUNKS
    for start in range(0, packed, size):
        spread(start, factor_ref[start : start + size, :], factor_ref[packed + start : packed + start + size, :])
    extra = projected_ref.shape[0] // 2
    spread(packed, projected_ref[:extra, :], projected_ref[extra:, :])


def folded(whole):
    half = whole.shape[0] // 4

    def block(i, j):
        return whole[i * half : (i + 1) * half, j * half : (j + 1) * half]

    return jnp.concatenate(
        [
            jnp.concatenate([block(0, 0) + block(1, 1), block(0, 2) + block(1, 3)], 1),
            jnp.concatenate([block(2, 0) + block(3, 1), block(2, 2) + block(3, 3)], 1),
        ],
        0,
    )


def second_gram_body(packed, count, *refs):
    refs, out_ref = refs[:-1], refs[-1]
    odd_refs, even_refs = refs[:count], refs[count:]
    size = packed // CHUNKS
    width = 2 * refs[0].shape[1]
    total = jnp.zeros((width, 2 * width), f32)
    for start in range(0, packed, size):
        high, low = split(
            jnp.concatenate([part(odd_refs, start, size), part(even_refs, start, size)], 1)
        )
        total += dot_rows(high, jnp.concatenate([high, low], 1))
    cross = folded(total[:, width:])
    gram = folded(total[:, :width]) + (cross + cross.T)
    gram = jnp.where(blk_index() % 2 == 1, swapped_rows(swapped_cols(gram)), gram)
    out_ref[...] = packed_gram(gram)


def second_solve_body(rounds, own_ref, other_ref, partner_ref, sign_ref, odd_ref, even_ref):
    gram = unpacked_gram(own_ref[...] + other_ref[...])
    width = gram.shape[0]
    half = width // 2
    ((settled, turn),) = solve(
        [(gram, identity_of(width))], round_of(partner_ref, 1, rounds), round_of(sign_ref, 1, rounds)
    )
    top = jnp.concatenate([tall(turn[:, :half]), tall(settled[:half, :half])], 0)
    bottom = jnp.concatenate([tall(turn[:, half:]), tall(settled[half:, half:])], 0)
    take_top = top_goes_odd()
    odd_ref[...] = jnp.where(take_top, top, bottom)
    even_ref[...] = jnp.where(take_top, bottom, top)


def cross_body(packed, extra, final, odd_far, odd_own, even_own, even_far, even_once, *refs):
    before_refs, out_ref = refs[:-1], refs[-1]
    width = odd_own.shape[1]
    half = width // 2
    position = blk_index()
    at_edge = jnp.logical_or(position == 0, position == final)

    def sides(start, end):
        odd_side = jnp.where(at_edge, even_once[start:end, :], odd_far[start:end, :])
        return (
            jnp.concatenate([odd_side, odd_own[start:end, :]], 1),
            jnp.concatenate([even_own[start:end, :], even_far[start:end, :]], 1),
        )

    size = packed // CHUNKS
    rows = odd_own.shape[0] - extra
    total = jnp.zeros((2 * width, 2 * width), f32)
    for start in range(0, rows, size):
        left, right = sides(start, start + size)
        left_high, left_low = split(left)
        right_high, right_low = split(right)
        total += dot_rows(
            jnp.concatenate([left_high, left_high, left_low], 0),
            jnp.concatenate([right_high, right_low, right_high], 0),
        )
    total = folded(total)
    for ref in before_refs:
        total += ref[...]
    out_ref[:width, :] = total
    if extra:
        for side, value in enumerate(sides(rows, rows + extra)):
            start = width + side * 2 * extra
            out_ref[start : start + extra, :half] = value[:, :half]
            out_ref[start : start + extra, half:] = value[:, width : width + half]
            out_ref[start + extra : start + 2 * extra, :half] = value[:, half:width]
            out_ref[start + extra : start + 2 * extra, half:] = value[:, width + half :]


def combine_body(final, cross_ref, odd_ref, even_ref, out_ref):
    width = cross_ref.shape[1]
    half = width // 2
    count = (cross_ref.shape[0] - width) // 2
    position = blk_index()
    odd = position % 2 == 1
    at_edge = jnp.logical_or(position == 0, position == final)
    odd_turn, even_turn = square(odd_ref[:half, :]), square(even_ref[:half, :])
    odd_turn = jnp.where(jnp.logical_xor(odd, at_edge), swapped_rows(odd_turn), odd_turn)
    even_turn = jnp.where(odd, swapped_rows(even_turn), even_turn)
    odd_stack, even_stack = stacked(odd_turn), stacked(even_turn)
    high, low = split(rotated(cross_ref[:width, :], even_stack))
    cross = dot_rows(odd_stack, jnp.concatenate([high, low, high], 0))
    share = 0.25
    odd_gram = square(odd_ref[half:, :]) * share
    even_gram = square(even_ref[half:, :]) * share
    odd_samples = rotated(cross_ref[width : width + count, :], odd_stack)
    even_samples = rotated(cross_ref[width + count :, :], even_stack)
    first = jnp.where(odd, even_gram, odd_gram)
    second = jnp.where(odd, odd_gram, even_gram)
    cross = jnp.where(odd, cross.T, cross)
    samples = jnp.concatenate(
        [jnp.where(odd, even_samples, odd_samples), jnp.where(odd, odd_samples, even_samples)], 1
    )
    first_core = lax.axis_index("rows") % 2 == 0
    out_ref[:count, :] = jnp.where(first_core, samples, 0.0)
    out_ref[count : 2 * count, :] = jnp.where(first_core, 0.0, samples)
    count = 2 * count
    out_ref[count : count + half, :half] = first
    out_ref[count : count + half, half:] = cross
    out_ref[count + half : count + half + half // 2, :] = tall(second)
    out_ref[count + half + half // 2 :, :] = jnp.zeros((8, width), f32)


def last_solve_body(
    rounds, final, odd_ref, odd_other_ref, even_ref, even_other_ref, partner_ref, sign_ref, sums_ref, squares_ref
):
    kept = odd_ref.shape[0]
    wholes = [odd_ref[...] + odd_other_ref[...], even_ref[:kept, :] + even_other_ref[:kept, :]]
    width = wholes[0].shape[1]
    half = width // 2
    samples = wholes[0].shape[0] - width * 3 // 4
    solved = solve(
        [(unpacked_gram(whole[samples:]), whole[:samples]) for whole in wholes],
        round_of(partner_ref, 2, rounds),
        round_of(sign_ref, 2, rounds),
        "sums",
    )
    takes = [odd_takes_top(final), even_takes_top()]
    halves = []
    for (sums, projected), take_top in zip(solved, takes):
        squares = jnp.sum(projected * projected, axis=0, keepdims=True) * (1.0 / samples)
        both = jnp.concatenate([sums, squares], 0)
        halves.append(jnp.where(take_top, both[:, :half], both[:, half:]))
    odd = blk_index() % 2 == 1
    first = jnp.where(odd, halves[1], halves[0])
    second = jnp.where(odd, halves[0], halves[1])
    result = jnp.concatenate([first, second], 1)
    sums_ref[...] = result[0:1]
    squares_ref[...] = result[1:2]


def odd_partner(position, count):
    partner = position - 1 if position % 2 == 0 else position + 1
    return partner if 0 <= partner < count else position


def even_partner(position):
    return position + 1 if position % 2 == 0 else position - 1


def via_odd(value, closed):
    count = lax.axis_size("blk")
    pairs = [(i, odd_partner(i, count)) for i in range(count)]
    return lax.ppermute(value, "blk", [pair for pair in pairs if closed or pair[0] != pair[1]])


def via_even(value):
    count = lax.axis_size("blk")
    return lax.ppermute(value, "blk", [(i, even_partner(i)) for i in range(count)])


def both_chips(value, partner_of):
    count, rows = lax.axis_size("blk"), lax.axis_size("rows")
    pairs = []
    for i in range(count):
        for row in range(rows):
            chip, core = row // 2, row % 2
            pairs.append((i * rows + row, partner_of(i) * rows + core * 2 + chip))
    mine = lax.ppermute(value, ("blk", "rows"), pairs)
    return mine, flipped(mine, 1)


def both_partners(value):
    count = lax.axis_size("blk")
    even = both_chips(value, even_partner)
    odd = both_chips(value[:-8], lambda i: odd_partner(i, count))
    return odd + even


def flipped(value, bit):
    return lax.ppermute(value, "rows", [(i, i ^ bit) for i in range(lax.axis_size("rows"))])


def on_device(factor_cols, basis_cols, samples, pairing):
    width = factor_cols.shape[1]
    packed = factor_cols.shape[0] // 2
    sample_count = samples.shape[0]
    extra = sample_count // 4
    rounds, steps = pairing.shape[0], pairing.shape[1]
    final = lax.axis_size("blk") - 1

    gram = first_gram(factor_cols)
    paired = gram + flipped(gram, 1)
    pairing, paired = lax.optimization_barrier((pairing, paired))
    mine, theirs, partner, sign = project(samples, basis_cols, pairing.reshape(rounds * steps, width))
    theirs, arrived = lax.optimization_barrier((theirs, flipped(paired, 2)))
    projected = mine + flipped(theirs, 1)
    turn = call(lambda *refs: first_solve_body(rounds, *refs), shape(width, width), [VMEM] * 4, 4 * 10**9)(
        paired, arrived, partner, sign
    )
    first, second = packed * CUT // CHUNKS, packed * (CHUNKS - CUT) // CHUNKS + extra
    pieces = [shape(first, width), shape(second, width)]
    count = len(pieces)
    sent = call(
        lambda *refs: rotate_body(count, *refs), tuple(pieces + pieces), [VMEM] * 3
    )(factor_cols, projected, turn)
    to_odd, to_even = sent[:count], sent[count:]
    even_once = [via_even(value) for value in to_even]
    odd_once = [via_odd(value, True) for value in to_odd]
    odd_twice = [via_odd(value, False) for value in even_once]
    even_twice = [via_even(value) for value in odd_once]
    gram = call(
        lambda *refs: second_gram_body(packed, count, *refs),
        shape(width * 3 // 4, width),
        [VMEM] * (2 * count),
    )(*odd_once, *even_once)
    paired = gram + flipped(gram, 1)
    for_odd, for_even = call(
        lambda *refs: second_solve_body(rounds, *refs),
        (shape(width * 3 // 4, width), shape(width * 3 // 4, width)),
        [VMEM] * 4,
    )(paired, flipped(paired, 2), partner, sign)
    groups = [list(group) for group in zip(odd_twice, to_odd, to_even, even_twice, even_once)]
    groups[0][1], for_odd, for_even = lax.optimization_barrier((groups[0][1], for_odd, for_even))
    cross = call(lambda *refs: cross_body(packed, 0, final, *refs), shape(width, width), [VMEM] * 5)(*groups[0])
    from_even = via_even(for_even)
    from_odd = via_odd(for_odd, True)
    cross = call(
        lambda *refs: cross_body(packed, extra, final, *refs), shape(width + sample_count, width), [VMEM] * 6
    )(*groups[1], cross)
    whole = call(
        lambda *refs: combine_body(final, *refs), shape(width * 3 // 4 + sample_count + 8, width), [VMEM] * 3
    )(cross, from_odd, from_even)
    paired = whole + flipped(whole, 1)
    sums, squares = call(
        lambda *refs: last_solve_body(rounds, final, *refs),
        (shape(1, width), shape(1, width)),
        [VMEM] * 6,
    )(*both_partners(paired), partner, sign)
    return (sums.reshape(width), squares.reshape(width))


def solution(mesh):
    in_specs = (P("rows", "blk"), P("rows", "blk"), P(None, "rows"), P())
    out_specs = (P("blk"), P("blk"))
    return jax.shard_map(
        on_device, mesh=mesh, in_specs=in_specs, out_specs=out_specs, check_vma=False
    )
```

```python
import jax
import jax.numpy as jnp
from jax import lax
from jax.experimental import pallas as pl
from jax.experimental.pallas import tpu as pltpu
from jax.sharding import PartitionSpec as P

f32 = jnp.float32
bf16 = jnp.bfloat16
i32 = jnp.int32
VMEM = pl.BlockSpec(memory_space=pltpu.VMEM)
params = pltpu.CompilerParams(vmem_limit_bytes=24 * 1024 * 1024)
CHUNKS = 8
CUT = 5
large_params = pltpu.CompilerParams(vmem_limit_bytes=52 * 1024 * 1024)


def split(value):
    high = value.astype(bf16)
    low = (value - high.astype(f32)).astype(bf16)
    return high, low


def dot(left, right):
    return jnp.dot(left, right, preferred_element_type=f32)


def dot_rows(left, right):
    return lax.dot_general(left, right, (((0,), (0,)), ((), ())), preferred_element_type=f32)


def rotated(left, right):
    high, low = split(left)
    return dot(jnp.concatenate([high, low, high], 1), right)


def stacked(right):
    high, low = split(right)
    return jnp.concatenate([high, high, low], 0)


def chunks_of(rows, most):
    size = min(rows, most)
    return rows // size, size


def part(refs, start, size):
    for ref in refs:
        if start < ref.shape[0]:
            return ref[start : start + size, :]
        start -= ref.shape[0]


def put(refs, start, value):
    for ref in refs:
        if start < ref.shape[0]:
            ref[start : start + value.shape[0], :] = value
            return
        start -= ref.shape[0]


def call(body, out_shape, in_specs):
    return pl.pallas_call(
        body,
        out_shape=out_shape,
        in_specs=in_specs,
        out_specs=jax.tree.map(lambda _: VMEM, out_shape),
        compiler_params=params,
        cost_estimate=pl.CostEstimate(flops=1, bytes_accessed=1, transcendentals=0),
    )


def shape(*dims, dtype=f32):
    return jax.ShapeDtypeStruct(dims, dtype)


def swapped_rows(value):
    half = value.shape[0] // 2
    return jnp.concatenate([value[half:], value[:half]], 0)


def swapped_cols(value):
    half = value.shape[1] // 2
    return jnp.concatenate([value[:, half:], value[:, :half]], 1)


def fetches(source, target, sems, first, cut):
    count, size = chunks_of(target.shape[cut], 1024)
    copies = []
    for i in range(count):
        part = (slice(None),) * cut + (pl.ds(i * size, size),)
        copies.append(pltpu.make_async_copy(source.at[part], target.at[part], sems.at[first + i]))
    return copies, size


def tall(value):
    quarter = value.shape[0] // 2
    return jnp.concatenate([value[:quarter], value[quarter:]], 1)


def square(value):
    half = value.shape[1] // 2
    return jnp.concatenate([value[:, :half], value[:, half:]], 0)


def packed_gram(gram):
    half = gram.shape[0] // 2
    return jnp.concatenate([gram[:half], tall(gram[half:, half:])], 0)


def unpacked_gram(value):
    half = value.shape[1] // 2
    across = value[:half, half:]
    return jnp.concatenate(
        [value[:half], jnp.concatenate([across.T, square(value[half:])], 1)], 0
    )


def first_gram_body(factor_hbm, out_ref, factor_ref, sems):
    width = factor_ref.shape[1]
    copies, size = fetches(factor_hbm, factor_ref, sems, 0, 0)
    for copy in copies:
        copy.start()
    total = jnp.zeros((width, 2 * width), f32)
    for i, copy in enumerate(copies):
        copy.wait()
        high, low = split(factor_ref[i * size : (i + 1) * size, :])
        total += dot_rows(high, jnp.concatenate([high, low], 1))
    cross = total[:, width:]
    out_ref[...] = packed_gram(total[:, :width] + (cross + cross.T))


def first_gram(factor_cols):
    rows, width = factor_cols.shape
    return pl.pallas_call(
        first_gram_body,
        out_shape=shape(width * 3 // 4, width),
        in_specs=[pl.BlockSpec(memory_space=pl.ANY)],
        out_specs=VMEM,
        scratch_shapes=[
            pltpu.VMEM((rows, width), f32),
            pltpu.SemaphoreType.DMA((chunks_of(rows, 1024)[0],)),
        ],
        compiler_params=large_params,
    )(factor_cols)


def project_body(samples_hbm, basis_hbm, order_ref, out_ref, partner_ref, sign_ref, samples_ref, basis_ref, sems):
    width = basis_ref.shape[1]
    lefts, size = fetches(samples_hbm, samples_ref, sems, 0, 1)
    rights, size = fetches(basis_hbm, basis_ref, sems, len(lefts), 0)
    for left, right in zip(lefts, rights):
        left.start()
        right.start()

    lines = order_ref.shape[0]
    order = order_ref[...]
    lane = lax.broadcasted_iota(i32, (lines, width), 1)
    ahead = jnp.concatenate([order[:, 1:], order[:, :1]], 1)
    behind = jnp.concatenate([order[:, -1:], order[:, :-1]], 1)
    even = lane % 2 == 0
    other = jnp.where(even, ahead, behind + width)
    filler = jnp.zeros((width - lines, width), i32)
    order = jnp.concatenate([order, filler], 0).T
    other = jnp.concatenate([other, filler], 0).T
    column = lax.broadcasted_iota(i32, (width, width), 1)
    found = []
    for line in range(lines):
        hits = jnp.where(order[:, line : line + 1] == column, other[:, line : line + 1], 0)
        found.append(jnp.sum(hits, axis=0, keepdims=True))
    found = jnp.concatenate(found, 0)
    first = found < width
    partner_ref[...] = jnp.where(first, found, found - width)
    sign_ref[...] = jnp.where(first, 1.0, -1.0).astype(f32)

    total = jnp.zeros(out_ref.shape, f32)
    for i, (left, right) in enumerate(zip(lefts, rights)):
        left.wait()
        right.wait()
        left_high, left_low = split(samples_ref[:, i * size : (i + 1) * size])
        right_high, right_low = split(basis_ref[i * size : (i + 1) * size, :])
        both = dot(left_high, jnp.concatenate([right_high, right_low], 1))
        total += both[:, :width] + both[:, width:] + dot(left_low, right_high)
    out_ref[...] = total


def project(samples, basis_cols, order):
    rows, width = basis_cols.shape
    lines = order.shape[0]
    return pl.pallas_call(
        project_body,
        out_shape=(
            shape(samples.shape[0], width),
            shape(lines, width, dtype=i32),
            shape(lines, width),
        ),
        in_specs=[pl.BlockSpec(memory_space=pl.ANY)] * 2 + [VMEM],
        out_specs=(VMEM, VMEM, VMEM),
        scratch_shapes=[
            pltpu.VMEM(samples.shape, f32),
            pltpu.VMEM((rows, width), f32),
            pltpu.SemaphoreType.DMA((2 * chunks_of(rows, 1024)[0],)),
        ],
        compiler_params=large_params,
    )(samples, basis_cols, order)


def lanes(value, index):
    return jnp.take_along_axis(value, index, axis=1, mode="promise_in_bounds")


def eye_of(width):
    row_id = lax.broadcasted_iota(i32, (width, width), 0)
    col_id = lax.broadcasted_iota(i32, (width, width), 1)
    return row_id == col_id


def column_sums(value):
    total = jnp.sum(value.reshape(-1, 8, value.shape[1]), axis=0)
    for shift in (4, 2, 1):
        total += pltpu.roll(total, shift, 0)
    return total


def scaled(value, factor):
    return (value.reshape(-1, 8, value.shape[1]) * factor[None]).reshape(value.shape)


def turn_step(settled, carried, eye, index, facing, sign, last):
    swapped = lanes(settled, index)
    own = column_sums(jnp.where(eye, settled, 0.0))
    other = column_sums(jnp.where(facing, swapped, 0.0))
    up = column_sums(jnp.where(eye, swapped, 0.0)) + column_sums(jnp.where(facing, settled, 0.0))
    across = sign * (own - other)
    scale = jnp.maximum(jnp.abs(across), jnp.abs(up))
    found = scale > 0.0
    shrink = 1.0 / jnp.where(found, scale, 1.0)
    level = jnp.where(found, across * shrink, 1.0)
    slope = up * shrink
    inverse = lax.rsqrt(level * level + slope * slope)
    major_square = 0.5 + 0.5 * jnp.abs(level) * inverse
    against = lax.rsqrt(major_square)
    major = major_square * against
    minor = 0.5 * jnp.abs(slope) * inverse * against
    ahead = level >= 0.0
    cosine = jnp.where(ahead, major, minor)
    sine = jnp.where(ahead, minor, major)
    sine = jnp.where(slope < 0.0, -sine, sine) * sign
    if carried is None:
        carried = scaled(jnp.where(eye, 1.0, 0.0), cosine) + scaled(jnp.where(facing, 1.0, 0.0), sine)
    else:
        carried = scaled(carried, cosine) + scaled(lanes(carried, index), sine)
    if last == "turn":
        return None, carried
    if last == "sums":
        sums = own * (cosine * cosine) + other * (sine * sine) + up * (cosine * sine)
        return sums[0:1], carried
    turned = (scaled(settled, cosine) + scaled(swapped, sine)).T
    return scaled(turned, cosine) + scaled(lanes(turned, index), sine), carried


def solve(problems, partners, signs, last=None):
    width = problems[0][0].shape[0]
    eye = eye_of(width)
    row_id = lax.broadcasted_iota(i32, (width, width), 0)
    for step in range(partners.shape[0]):
        sign = jnp.broadcast_to(signs[step : step + 1, :], (8, width))
        index = jnp.broadcast_to(partners[step : step + 1, :], (width, width))
        ending = last if step == partners.shape[0] - 1 else None
        problems = [turn_step(*problem, eye, index, row_id == index, sign, ending) for problem in problems]
    return problems


def round_of(ref, index, rounds):
    steps = ref.shape[0] // rounds
    return ref[index * steps : (index + 1) * steps, :]


def blk_index():
    return lax.axis_index("blk").astype(i32)


def top_goes_odd():
    position = blk_index()
    return jnp.logical_or(position % 2 == 1, position == 0)


def odd_takes_top(final):
    position = blk_index()
    return jnp.logical_or(position % 2 == 0, position == final)


def even_takes_top():
    position = blk_index()
    return jnp.logical_and(position % 2 == 1, position != 1)


def identity_of(width):
    return jnp.where(eye_of(width), 1.0, 0.0).astype(f32)


def first_solve_body(rounds, own_ref, other_ref, partner_ref, sign_ref, turn_ref):
    gram = unpacked_gram(own_ref[...] + other_ref[...])
    ((_, turn_ref[...]),) = solve(
        [(gram, None)],
        round_of(partner_ref, 0, rounds),
        round_of(sign_ref, 0, rounds),
        "turn",
    )


def rotate_body(odd_count, factor_ref, projected_ref, turn_ref, *out_refs):
    odd_refs, even_refs = out_refs[:odd_count], out_refs[odd_count:]
    width = factor_ref.shape[1]
    half = width // 2
    packed = factor_ref.shape[0] // 2
    turn = turn_ref[...]
    turn = jnp.where(top_goes_odd(), turn, swapped_cols(turn))
    for_odd, for_even = turn[:, :half], turn[:, half:]
    empty = jnp.zeros_like(for_odd)
    weights = jnp.concatenate(
        [
            jnp.concatenate([for_odd, empty, for_even, empty], 1),
            jnp.concatenate([empty, for_odd, empty, for_even], 1),
        ],
        0,
    )
    weights = stacked(weights)

    def spread(start, lower, upper):
        result = rotated(jnp.concatenate([lower, upper], 1), weights)
        put(odd_refs, start, result[:, :width])
        put(even_refs, start, result[:, width:])

    size = packed // CHUNKS
    for start in range(0, packed, size):
        spread(start, factor_ref[start : start + size, :], factor_ref[packed + start : packed + start + size, :])
    extra = projected_ref.shape[0] // 2
    spread(packed, projected_ref[:extra, :], projected_ref[extra:, :])


def folded(whole):
    half = whole.shape[0] // 4

    def block(i, j):
        return whole[i * half : (i + 1) * half, j * half : (j + 1) * half]

    return jnp.concatenate(
        [
            jnp.concatenate([block(0, 0) + block(1, 1), block(0, 2) + block(1, 3)], 1),
            jnp.concatenate([block(2, 0) + block(3, 1), block(2, 2) + block(3, 3)], 1),
        ],
        0,
    )


def second_gram_body(packed, count, *refs):
    refs, out_ref = refs[:-1], refs[-1]
    odd_refs, even_refs = refs[:count], refs[count:]
    size = packed // CHUNKS
    width = 2 * refs[0].shape[1]
    total = jnp.zeros((width, 2 * width), f32)
    for start in range(0, packed, size):
        high, low = split(
            jnp.concatenate([part(odd_refs, start, size), part(even_refs, start, size)], 1)
        )
        total += dot_rows(high, jnp.concatenate([high, low], 1))
    cross = folded(total[:, width:])
    gram = folded(total[:, :width]) + (cross + cross.T)
    gram = jnp.where(blk_index() % 2 == 1, swapped_rows(swapped_cols(gram)), gram)
    out_ref[...] = packed_gram(gram)


def second_solve_body(rounds, own_ref, other_ref, partner_ref, sign_ref, odd_ref, even_ref):
    gram = unpacked_gram(own_ref[...] + other_ref[...])
    width = gram.shape[0]
    half = width // 2
    ((settled, turn),) = solve(
        [(gram, None)], round_of(partner_ref, 1, rounds), round_of(sign_ref, 1, rounds)
    )
    top = jnp.concatenate([tall(turn[:, :half]), tall(settled[:half, :half])], 0)
    bottom = jnp.concatenate([tall(turn[:, half:]), tall(settled[half:, half:])], 0)
    take_top = top_goes_odd()
    odd_ref[...] = jnp.where(take_top, top, bottom)
    even_ref[...] = jnp.where(take_top, bottom, top)


def cross_body(packed, extra, final, odd_far, odd_own, even_own, even_far, even_once, *refs):
    before_refs, out_ref = refs[:-1], refs[-1]
    width = odd_own.shape[1]
    half = width // 2
    position = blk_index()
    at_edge = jnp.logical_or(position == 0, position == final)

    def sides(start, end):
        odd_side = jnp.where(at_edge, even_once[start:end, :], odd_far[start:end, :])
        return (
            jnp.concatenate([odd_side, odd_own[start:end, :]], 1),
            jnp.concatenate([even_own[start:end, :], even_far[start:end, :]], 1),
        )

    size = packed // CHUNKS
    rows = odd_own.shape[0] - extra
    total = jnp.zeros((2 * width, 2 * width), f32)
    for start in range(0, rows, size):
        left, right = sides(start, start + size)
        left_high, left_low = split(left)
        right_high, right_low = split(right)
        total += dot_rows(
            jnp.concatenate([left_high, left_high, left_low], 0),
            jnp.concatenate([right_high, right_low, right_high], 0),
        )
    total = folded(total)
    for ref in before_refs:
        total += ref[...]
    out_ref[:width, :] = total
    if extra:
        for side, value in enumerate(sides(rows, rows + extra)):
            start = width + side * 2 * extra
            out_ref[start : start + extra, :half] = value[:, :half]
            out_ref[start : start + extra, half:] = value[:, width : width + half]
            out_ref[start + extra : start + 2 * extra, :half] = value[:, half:width]
            out_ref[start + extra : start + 2 * extra, half:] = value[:, width + half :]


def combine_body(final, cross_ref, odd_ref, even_ref, out_ref):
    width = cross_ref.shape[1]
    half = width // 2
    count = (cross_ref.shape[0] - width) // 2
    position = blk_index()
    odd = position % 2 == 1
    at_edge = jnp.logical_or(position == 0, position == final)
    odd_turn, even_turn = square(odd_ref[:half, :]), square(even_ref[:half, :])
    odd_turn = jnp.where(jnp.logical_xor(odd, at_edge), swapped_rows(odd_turn), odd_turn)
    even_turn = jnp.where(odd, swapped_rows(even_turn), even_turn)
    odd_stack, even_stack = stacked(odd_turn), stacked(even_turn)
    high, low = split(rotated(cross_ref[:width, :], even_stack))
    cross = dot_rows(odd_stack, jnp.concatenate([high, low, high], 0))
    share = 0.25
    odd_gram = square(odd_ref[half:, :]) * share
    even_gram = square(even_ref[half:, :]) * share
    odd_samples = rotated(cross_ref[width : width + count, :], odd_stack)
    even_samples = rotated(cross_ref[width + count :, :], even_stack)
    first = jnp.where(odd, even_gram, odd_gram)
    second = jnp.where(odd, odd_gram, even_gram)
    cross = jnp.where(odd, cross.T, cross)
    out_ref[:count, :half] = jnp.where(odd, even_samples, odd_samples)
    out_ref[:count, half:] = jnp.where(odd, odd_samples, even_samples)
    out_ref[count : count + half, :half] = first
    out_ref[count : count + half, half:] = cross
    out_ref[count + half : count + half + half // 2, :] = tall(second)
    out_ref[count + half + half // 2 :, :] = jnp.zeros((8, width), f32)


def last_solve_body(
    rounds, final, odd_ref, odd_other_ref, even_ref, even_other_ref, partner_ref, sign_ref, sums_ref, squares_ref
):
    kept = odd_ref.shape[0]
    wholes = [odd_ref[...] + odd_other_ref[...], even_ref[:kept, :] + even_other_ref[:kept, :]]
    width = wholes[0].shape[1]
    half = width // 2
    samples = wholes[0].shape[0] - width * 3 // 4
    solved = solve(
        [(unpacked_gram(whole[samples:]), whole[:samples]) for whole in wholes],
        round_of(partner_ref, 2, rounds),
        round_of(sign_ref, 2, rounds),
        "sums",
    )
    takes = [odd_takes_top(final), even_takes_top()]
    halves = []
    for (sums, projected), take_top in zip(solved, takes):
        squares = jnp.sum(projected * projected, axis=0, keepdims=True) * (1.0 / samples)
        both = jnp.concatenate([sums, squares], 0)
        halves.append(jnp.where(take_top, both[:, :half], both[:, half:]))
    odd = blk_index() % 2 == 1
    first = jnp.where(odd, halves[1], halves[0])
    second = jnp.where(odd, halves[0], halves[1])
    result = jnp.concatenate([first, second], 1)
    sums_ref[...] = result[0:1]
    squares_ref[...] = result[1:2]


def odd_partner(position, count):
    partner = position - 1 if position % 2 == 0 else position + 1
    return partner if 0 <= partner < count else position


def even_partner(position):
    return position + 1 if position % 2 == 0 else position - 1


def via_odd(value, closed):
    count = lax.axis_size("blk")
    pairs = [(i, odd_partner(i, count)) for i in range(count)]
    return lax.ppermute(value, "blk", [pair for pair in pairs if closed or pair[0] != pair[1]])


def via_even(value):
    count = lax.axis_size("blk")
    return lax.ppermute(value, "blk", [(i, even_partner(i)) for i in range(count)])


def both_chips(value, partner_of):
    count, rows = lax.axis_size("blk"), lax.axis_size("rows")
    pairs = []
    for i in range(count):
        for row in range(rows):
            chip, core = row // 2, row % 2
            pairs.append((i * rows + row, partner_of(i) * rows + core * 2 + chip))
    mine = lax.ppermute(value, ("blk", "rows"), pairs)
    return mine, flipped(mine, 1)


def both_partners(value):
    count = lax.axis_size("blk")
    even = both_chips(value, even_partner)
    odd = both_chips(value[:-8], lambda i: odd_partner(i, count))
    return odd + even


def flipped(value, bit):
    return lax.ppermute(value, "rows", [(i, i ^ bit) for i in range(lax.axis_size("rows"))])


def on_device(factor_cols, basis_cols, samples, pairing):
    width = factor_cols.shape[1]
    packed = factor_cols.shape[0] // 2
    sample_count = samples.shape[0]
    extra = sample_count // 2
    rounds, steps = pairing.shape[0], pairing.shape[1]
    final = lax.axis_size("blk") - 1

    gram = first_gram(factor_cols)
    paired = gram + flipped(gram, 1)
    pairing, paired = lax.optimization_barrier((pairing, paired))
    projected, partner, sign = project(samples, basis_cols, pairing.reshape(rounds * steps, width))
    turn = call(lambda *refs: first_solve_body(rounds, *refs), shape(width, width), [VMEM] * 4)(
        paired, flipped(paired, 2), partner, sign
    )
    first, second = packed * CUT // CHUNKS, packed * (CHUNKS - CUT) // CHUNKS + extra
    pieces = [shape(first, width), shape(second, width)]
    count = len(pieces)
    sent = call(
        lambda *refs: rotate_body(count, *refs), tuple(pieces + pieces), [VMEM] * 3
    )(factor_cols, projected, turn)
    to_odd, to_even = sent[:count], sent[count:]
    even_once = [via_even(value) for value in to_even]
    odd_once = [via_odd(value, True) for value in to_odd]
    odd_twice = [via_odd(value, False) for value in even_once]
    even_twice = [via_even(value) for value in odd_once]
    gram = call(
        lambda *refs: second_gram_body(packed, count, *refs),
        shape(width * 3 // 4, width),
        [VMEM] * (2 * count),
    )(*odd_once, *even_once)
    paired = gram + flipped(gram, 1)
    for_odd, for_even = call(
        lambda *refs: second_solve_body(rounds, *refs),
        (shape(width * 3 // 4, width), shape(width * 3 // 4, width)),
        [VMEM] * 4,
    )(paired, flipped(paired, 2), partner, sign)
    groups = [list(group) for group in zip(odd_twice, to_odd, to_even, even_twice, even_once)]
    groups[0][1], for_odd, for_even = lax.optimization_barrier((groups[0][1], for_odd, for_even))
    cross = call(lambda *refs: cross_body(packed, 0, final, *refs), shape(width, width), [VMEM] * 5)(*groups[0])
    from_even = via_even(for_even)
    from_odd = via_odd(for_odd, True)
    cross = call(
        lambda *refs: cross_body(packed, extra, final, *refs), shape(width + 2 * sample_count, width), [VMEM] * 6
    )(*groups[1], cross)
    whole = call(
        lambda *refs: combine_body(final, *refs), shape(width * 3 // 4 + sample_count + 8, width), [VMEM] * 3
    )(cross, from_odd, from_even)
    paired = whole + flipped(whole, 1)
    sums, squares = call(
        lambda *refs: last_solve_body(rounds, final, *refs),
        (shape(1, width), shape(1, width)),
        [VMEM] * 6,
    )(*both_partners(paired), partner, sign)
    return (sums.reshape(width), squares.reshape(width))


def solution(mesh):
    in_specs = (P("rows", "blk"), P("rows", "blk"), P(None, "rows"), P())
    out_specs = (P("blk"), P("blk"))
    return jax.shard_map(
        on_device, mesh=mesh, in_specs=in_specs, out_specs=out_specs, check_vma=False
    )
```
